256 devices in a mesh: seq: 32 (over z, y_hi, core), res: 8 (over x, y_lo).
Axes of the slice: x: 4, y: 4 (y_hi: 2, y_lo: 2; y = y_hi * 2 + y_lo), z: 8, core: 2. Of those that a mesh axis runs over, the one named last changes fastest.
Arguments:
- homolog_embedding: bfloat16 [512, 1024, 256], P('seq', 'res'), may hold values from -6 to 6
- pair_features: bfloat16 [1024, 1024, 128], P('seq', 'res'), may hold values from -6 to 6
- row_present_mask: int32 [512], replicated, may hold values 0 or 1
- residue_keep_mask: int32 [1024], replicated, may hold values 0 or 1
- query_weight: bfloat16 [256, 256], replicated, may hold values from -64 to 64
- key_weight: bfloat16 [256, 256], replicated, may hold values from -1 to 1
- content_matrix: bfloat16 [256, 256], replicated, may hold values from -0.375 to 0.375
- sigmoid_switch_matrix: bfloat16 [256, 256], replicated, may hold values from -0.375 to 0.375
- focus_merge_matrix: bfloat16 [256, 256], replicated, may hold values from -0.375 to 0.375
- widening_matrix: bfloat16 [256, 1024], replicated, may hold values from -0.375 to 0.375
- narrowing_matrix: bfloat16 [1024, 256], replicated, may hold values from -0.1875 to 0.1875
- first_factor_matrix: bfloat16 [256, 32], replicated, may hold values from -0.375 to 0.375
- second_factor_matrix: bfloat16 [256, 32], replicated, may hold values from -0.375 to 0.375
- outer_product_weight: bfloat16 [1024, 128], replicated, may hold values from -1 to 1
- outer_product_bias: float32 [128], replicated, may hold values from -3 to 3
- pair_up_weight: bfloat16 [128, 512], replicated, may hold values from -0.5 to 0.5
- pair_down_weight: bfloat16 [512, 128], replicated, may hold values from -0.25 to 0.25
Outputs:
- msa_update: bfloat16 [512, 1024, 256], P('seq', 'res')
- pair_update: bfloat16 [1024, 1024, 128], P('seq', 'res')
The draws below stay inside these ranges and needn't reach their ends.
All inputs are finite; a program needn't handle non-finite values.
Results may differ from the reference program's by a relative error of at most 0.012.
Values may be sent and summed in bfloat16 or wider, within the bound.
No kernel may reach another device: no remote copies, remote signals or barrier semaphores. Data moves between devices by JAX's collectives and lax.ppermute only.
A program may use at most 64 MiB of HBM per device.

```python
import math
import jax
import jax.numpy as jnp
from jax import lax

EMBED_BREADTH = 256
C_Z = 128
FOCUS_NUMBER = 8
FOCUS_BREADTH = 32
COUPLING_DIM = 32
LAYER_HIDDEN = 1024
TRANS_Z = 512
HOMOLOG_NUMBER = 512
AMINO_NUMBER = 1024


def query_key_base(key):
    base_key = jax.random.fold_in(key, 7)
    asking_random_seed, lookup_random_seed = jax.random.split(base_key, 2)
    asking_piece = jax.random.normal(asking_random_seed, (EMBED_BREADTH, FOCUS_NUMBER * FOCUS_BREADTH), jnp.float32) / math.sqrt(EMBED_BREADTH)
    lookup_piece = jax.random.normal(lookup_random_seed, (EMBED_BREADTH, FOCUS_NUMBER * FOCUS_BREADTH), jnp.float32) / math.sqrt(EMBED_BREADTH)
    lookup_piece = jnp.clip(lookup_piece, -0.9, 0.9)
    asking_piece = jnp.clip(asking_piece, -0.9, 0.9)
    return (asking_piece, lookup_piece)


def draw_key_weight(key, part):
    asking_piece, lookup_piece = query_key_base(key)
    return lookup_piece.astype(jnp.bfloat16)


def draw_query_weight(key, part):
    asking_piece, lookup_piece = query_key_base(key)
    return asking_piece.astype(jnp.bfloat16)


def touch_ends(drawn, stream_key, least, high):
    longest = drawn.shape.index(max(drawn.shape))
    spots = []
    for shift in (0, 1):
        where = [jax.random.randint(jax.random.fold_in(stream_key, axis), (), 0, length) for axis, length in enumerate(drawn.shape)]
        where[longest] = (where[longest] + shift) % drawn.shape[longest]
        spots.append(tuple(where))
    return drawn.at[spots[0]].set(least).at[spots[1]].set(high)


def levels(rng, dims, shards, smallest, top_value):
    level, own = 1.0, jax.random.fold_in(rng, 6)
    for axis_at, shards_of in shards:
        heights = jnp.exp(jax.random.uniform(jax.random.fold_in(own, axis_at), (shards_of,), jnp.float32, smallest / len(shards), top_value / len(shards)))
        level = level * jnp.repeat(heights, dims[axis_at] // shards_of).reshape([-1 if axis == axis_at else 1 for axis in range(len(dims))])
    return level


def scatter_about(stream_key, extent, scale, reach, cuts=(), kind=jnp.bfloat16):
    drawn = scale * jax.random.normal(stream_key, extent, jnp.float32)
    if cuts:
        drawn = drawn * levels(stream_key, extent, cuts, -0.22, 0.18)
    return jnp.clip(drawn, -reach, reach).astype(kind)


def setup_inputs(seed: int = 0) -> dict:
    streams_of = jax.random.split(jax.random.key(seed), 18)
    return {
        "homolog_embedding": scatter_about(streams_of[0], (HOMOLOG_NUMBER, AMINO_NUMBER, EMBED_BREADTH), 1.0, 6.0, ((0, 32), (1, 8))),
        "pair_features": scatter_about(streams_of[1], (AMINO_NUMBER, AMINO_NUMBER, C_Z), 1.0, 6.0, ((0, 32), (1, 8))),
        "row_present_mask": touch_ends((jax.random.randint(streams_of[2], (HOMOLOG_NUMBER,), 0, 8) < 7).astype(jnp.int32), jax.random.fold_in(streams_of[2], 1), 0, 1),
        "residue_keep_mask": touch_ends((jax.random.randint(streams_of[3], (AMINO_NUMBER,), 0, 8) < 7).astype(jnp.int32), jax.random.fold_in(streams_of[3], 1), 0, 1),
        "query_weight": draw_query_weight(jax.random.fold_in(streams_of[17], 71), 0),
        "key_weight": draw_key_weight(jax.random.fold_in(streams_of[17], 71), 0),
        "content_matrix": scatter_about(streams_of[6], (EMBED_BREADTH, FOCUS_NUMBER * FOCUS_BREADTH), EMBED_BREADTH ** -0.5, 0.375),
        "sigmoid_switch_matrix": scatter_about(streams_of[7], (EMBED_BREADTH, FOCUS_NUMBER * FOCUS_BREADTH), EMBED_BREADTH ** -0.5, 0.375),
        "focus_merge_matrix": scatter_about(streams_of[8], (FOCUS_NUMBER * FOCUS_BREADTH, EMBED_BREADTH), (FOCUS_NUMBER * FOCUS_BREADTH) ** -0.5, 0.375),
        "widening_matrix": scatter_about(streams_of[9], (EMBED_BREADTH, LAYER_HIDDEN), EMBED_BREADTH ** -0.5, 0.375),
        "narrowing_matrix": scatter_about(streams_of[10], (LAYER_HIDDEN, EMBED_BREADTH), LAYER_HIDDEN ** -0.5, 0.1875),
        "first_factor_matrix": scatter_about(streams_of[11], (EMBED_BREADTH, COUPLING_DIM), EMBED_BREADTH ** -0.5, 0.375),
        "second_factor_matrix": scatter_about(streams_of[12], (EMBED_BREADTH, COUPLING_DIM), EMBED_BREADTH ** -0.5, 0.375),
        "outer_product_weight": scatter_about(streams_of[13], (COUPLING_DIM * COUPLING_DIM, C_Z), COUPLING_DIM ** -0.5, 1.0),
        "outer_product_bias": scatter_about(streams_of[14], (C_Z,), 0.5, 3.0, (), jnp.float32),
        "pair_up_weight": scatter_about(streams_of[15], (C_Z, TRANS_Z), C_Z ** -0.5, 0.5),
        "pair_down_weight": scatter_about(streams_of[16], (TRANS_Z, C_Z), TRANS_Z ** -0.5, 0.25),
    }


epsilon = 1e-05
mask_fill = 1000000000.0

def layer_norm(values):
    centre = values - lax.optimization_barrier(jnp.mean(values, axis=-1, keepdims=True))
    spread = lax.optimization_barrier(jnp.mean(centre * centre, axis=-1, keepdims=True))
    return centre * lax.rsqrt(spread + epsilon)

def column_delta(block, row_present_flags, attention_weights):
    query_weight, key_weight, content_matrix, sigmoid_switch_matrix, focus_merge_matrix, widening_matrix, narrowing_matrix, first_factor_matrix, second_factor_matrix = attention_weights
    row_count, item_count, channel_width = block.shape
    inputs = block.astype(jnp.float32)
    normed = layer_norm(inputs).astype(jnp.bfloat16)
    scaling = 1.0 / math.sqrt(FOCUS_BREADTH)
    queries = (jnp.dot(normed, query_weight, preferred_element_type=jnp.float32) * scaling).astype(jnp.bfloat16)
    queries = queries.reshape(row_count, item_count, FOCUS_NUMBER, FOCUS_BREADTH)
    keys_all = jnp.dot(normed, key_weight, preferred_element_type=jnp.float32).astype(jnp.bfloat16)
    keys_all = keys_all.reshape(row_count, item_count, FOCUS_NUMBER, FOCUS_BREADTH)
    values_all = jnp.dot(normed, content_matrix, preferred_element_type=jnp.float32).astype(jnp.bfloat16)
    values_all = values_all.reshape(row_count, item_count, FOCUS_NUMBER, FOCUS_BREADTH)
    gate_values = jax.nn.sigmoid(jnp.dot(normed, sigmoid_switch_matrix, preferred_element_type=jnp.float32))
    scores = jnp.einsum('skhd,tkhd->khst', queries.astype(jnp.float32), keys_all.astype(jnp.float32))
    scores = scores + ((row_present_flags - 1.0) * mask_fill)[None, None, None, :]
    peak_score = lax.optimization_barrier(jnp.max(scores, axis=-1, keepdims=True))
    exponent = jnp.exp(scores - peak_score)
    probs = (exponent / lax.optimization_barrier(jnp.sum(exponent, axis=-1, keepdims=True))).astype(jnp.bfloat16)
    attended = jnp.einsum('khst,tkhd->skhd', probs.astype(jnp.float32), values_all.astype(jnp.float32))
    attended = attended.reshape(row_count, item_count, FOCUS_NUMBER * FOCUS_BREADTH)
    gated = (gate_values * attended).astype(jnp.bfloat16)
    after_attn = (inputs + jnp.dot(gated, focus_merge_matrix, preferred_element_type=jnp.float32)).astype(jnp.bfloat16)
    normed_two = layer_norm(after_attn.astype(jnp.float32)).astype(jnp.bfloat16)
    hidden = jax.nn.relu(jnp.dot(normed_two, widening_matrix, preferred_element_type=jnp.float32)).astype(jnp.bfloat16)
    after_trans = (after_attn.astype(jnp.float32) + jnp.dot(hidden, narrowing_matrix, preferred_element_type=jnp.float32)).astype(jnp.bfloat16)
    normed_three = layer_norm(after_trans.astype(jnp.float32)).astype(jnp.bfloat16)
    row_scale = row_present_flags[:, None, None]
    left_proj = (jnp.dot(normed_three, first_factor_matrix, preferred_element_type=jnp.float32) * row_scale).astype(jnp.bfloat16)
    right_proj = (jnp.dot(normed_three, second_factor_matrix, preferred_element_type=jnp.float32) * row_scale).astype(jnp.bfloat16)
    return (after_trans, left_proj, right_proj)

def pair_block_update(left_rows, right_full, pair_block, norm_block, outer_product_weight, outer_product_bias, pair_up_weight, pair_down_weight):
    outer = jnp.einsum('sic,sje->ijce', left_rows.astype(jnp.float32), right_full.astype(jnp.float32)).astype(jnp.bfloat16)
    row_span, column_extent = norm_block.shape
    flat = outer.reshape(row_span, column_extent, COUPLING_DIM * COUPLING_DIM)
    projected = jnp.dot(flat, outer_product_weight, preferred_element_type=jnp.float32) + outer_product_bias
    outer_mean = projected / jnp.maximum(norm_block, 1.0)[:, :, None]
    pair_mid = (pair_block.astype(jnp.float32) + outer_mean).astype(jnp.bfloat16)
    normed = layer_norm(pair_mid.astype(jnp.float32)).astype(jnp.bfloat16)
    hidden = jax.nn.relu(jnp.dot(normed, pair_up_weight, preferred_element_type=jnp.float32)).astype(jnp.bfloat16)
    return (pair_mid.astype(jnp.float32) + jnp.dot(hidden, pair_down_weight, preferred_element_type=jnp.float32)).astype(jnp.bfloat16)

def reference(homolog_embedding, pair_features, row_present_mask, residue_keep_mask, query_weight, key_weight, content_matrix, sigmoid_switch_matrix, focus_merge_matrix, widening_matrix, narrowing_matrix, first_factor_matrix, second_factor_matrix, outer_product_weight, outer_product_bias, pair_up_weight, pair_down_weight):
    row_present_flags = row_present_mask.astype(jnp.float32)
    res_flags = residue_keep_mask.astype(jnp.float32)
    overall_rows, residue_total, channel_width = homolog_embedding.shape
    column_tile = math.gcd(residue_total, 64)
    group_view = homolog_embedding.reshape(overall_rows, residue_total // column_tile, column_tile, channel_width).transpose(1, 0, 2, 3)
    attention_weights = (query_weight, key_weight, content_matrix, sigmoid_switch_matrix, focus_merge_matrix, widening_matrix, narrowing_matrix, first_factor_matrix, second_factor_matrix)

    def group_size(block):
        return column_delta(block, row_present_flags, attention_weights)
    alignment_output, left_full, right_full = lax.map(group_size, group_view)
    alignment_output = alignment_output.transpose(1, 0, 2, 3).reshape(overall_rows, residue_total, channel_width)
    left_full = left_full.transpose(1, 0, 2, 3).reshape(overall_rows, residue_total, COUPLING_DIM)
    right_full = right_full.transpose(1, 0, 2, 3).reshape(overall_rows, residue_total, COUPLING_DIM)
    res_half = residue_keep_mask.astype(jnp.bfloat16)
    left_full = left_full * res_half[None, :, None]
    right_full = right_full * res_half[None, :, None]
    live_rows = jnp.sum(row_present_flags)
    row_block = math.gcd(residue_total, 32)
    block_count = residue_total // row_block
    left_groups = left_full.reshape(overall_rows, block_count, row_block, COUPLING_DIM).transpose(1, 0, 2, 3)
    pair_groups = pair_features.reshape(block_count, row_block, residue_total, C_Z)
    norm_groups = live_rows * res_flags.reshape(block_count, row_block)[:, :, None] * res_flags[None, None, :]

    def per_rows(pieces):
        left_rows, pair_block, norm_block = pieces
        return pair_block_update(left_rows, right_full, pair_block, norm_block, outer_product_weight, outer_product_bias, pair_up_weight, pair_down_weight)
    pair_output = lax.map(per_rows, (left_groups, pair_groups, norm_groups)).reshape(residue_total, residue_total, C_Z)
    return (alignment_output, pair_output)
```

```python
import math

import jax
import jax.numpy as jnp
from jax import lax
from jax.experimental import pallas as pl
from jax.experimental.pallas import tpu as pltpu
from jax.sharding import Mesh, PartitionSpec as P

HEADS = 8
HEAD = 32
COUPLING = 32
EPSILON = 1e-05
MASK_FILL = 1000000000.0
SEQ = ("z", "yh", "co")
RES = ("x", "yl")
F32 = jnp.float32
BF16 = jnp.bfloat16


def layer_norm(values):
    centre = values - jnp.mean(values, axis=-1, keepdims=True)
    spread = jnp.mean(centre * centre, axis=-1, keepdims=True)
    return centre * lax.rsqrt(spread + EPSILON)


def dot(a, b):
    return jnp.dot(a, b, preferred_element_type=F32)


def dot_nt(a, b):
    return lax.dot_general(a, b, (((1,), (1,)), ((), ())), preferred_element_type=F32)


def column_kernel(
    x_ref,
    fill_ref,
    row_col_ref,
    row_row_ref,
    keep_left_ref,
    keep_right_ref,
    wq_ref,
    wk_ref,
    wv_ref,
    wg_ref,
    wm_ref,
    w1_ref,
    w2_ref,
    f1_ref,
    f2_ref,
    out_ref,
    left_ref,
    right_ref,
    left_acc,
    right_acc,
    attended,
):
    step = pl.program_id(0)
    shape = x_ref.shape
    rows = shape[0] * shape[2]
    x = x_ref[:, 0].reshape(rows, shape[3]).astype(F32)
    normed = layer_norm(x).astype(BF16)
    normed_t = normed.T
    queries_t = (dot(wq_ref[...], normed_t) * (1.0 / math.sqrt(HEAD))).astype(BF16)
    values_t = dot(wv_ref[...], normed_t).astype(BF16)
    keys = dot(normed, wk_ref[...]).astype(BF16)
    fill = fill_ref[...]
    ones = jnp.ones((16, rows), BF16)
    for h in range(HEADS):
        cut = slice(h * HEAD, (h + 1) * HEAD)
        scores = dot(keys[:, cut], queries_t[cut]) + fill
        peak = jnp.max(scores, axis=0, keepdims=True)
        weights = jnp.exp(scores - peak).astype(BF16)
        summed = dot(jnp.concatenate([values_t[cut], ones], axis=0), weights)
        attended[cut, :] = summed[:HEAD] / summed[HEAD : HEAD + 1]
    gate = jax.nn.sigmoid(dot(normed, wg_ref[...]))
    gated = (gate * attended[...].T).astype(BF16)
    after = (x + dot(gated, wm_ref[...])).astype(BF16)
    after_wide = after.astype(F32)
    normed = layer_norm(after_wide).astype(BF16)
    hidden = jnp.maximum(dot(normed, w1_ref[...]), 0.0).astype(BF16)
    update = (after_wide + dot(hidden, w2_ref[...])).astype(BF16)
    out_ref[:, 0] = update.reshape(shape[0], shape[2], shape[3])
    normed = layer_norm(update.astype(F32)).astype(BF16)
    left = dot(normed, f1_ref[0])
    right = dot_nt(f2_ref[0], normed)

    @pl.when(step == 0)
    def _():
        left_acc[...] = left
        right_acc[...] = right

    @pl.when(step > 0)
    def _():
        left_acc[...] += left
        right_acc[...] += right

    @pl.when(step == pl.num_programs(0) - 1)
    def _():
        left_ref[...] = (left_acc[...] * row_col_ref[...] * keep_left_ref[...]).astype(BF16)
        right_ref[...] = (right_acc[...] * row_row_ref[...] * keep_right_ref[...]).astype(BF16)


def columns(x, fill, row_col, row_row, keep_left, keep_right, weights):
    sources, count, span, channels = x.shape
    rows = sources * span
    lanes = count * COUPLING

    def whole(a):
        return pl.BlockSpec(a.shape, lambda k, n=a.ndim: (0,) * n)

    column = pl.BlockSpec((sources, 1, span, channels), lambda k: (0, k, 0, 0))
    smalls = (fill, row_col, row_row, keep_left, keep_right)
    specs = [column] + [whole(a) for a in smalls] + [whole(w) for w in weights[:-2]]
    specs += [pl.BlockSpec((1,) + w.shape[1:], lambda k: (k, 0, 0)) for w in weights[-2:]]
    return pl.pallas_call(
        column_kernel,
        grid=(count,),
        in_specs=specs,
        out_specs=(
            column,
            pl.BlockSpec((rows, lanes), lambda k: (0, 0)),
            pl.BlockSpec((lanes, rows), lambda k: (0, 0)),
        ),
        out_shape=(
            jax.ShapeDtypeStruct(x.shape, BF16),
            jax.ShapeDtypeStruct((rows, lanes), BF16),
            jax.ShapeDtypeStruct((lanes, rows), BF16),
        ),
        scratch_shapes=[
            pltpu.VMEM((rows, lanes), F32),
            pltpu.VMEM((lanes, rows), F32),
            pltpu.VMEM((channels, rows), F32),
        ],
        compiler_params=pltpu.CompilerParams(
            dimension_semantics=("arbitrary",), vmem_limit_bytes=40 * 2**20
        ),
        cost_estimate=pl.CostEstimate(
            flops=12 * 10**9, bytes_accessed=4 * 2**20, transcendentals=9 * 10**6
        ),
    )(x, *smalls, *weights)


def pair_kernel(
    place_ref,
    pair_ref,
    scale_ref,
    own_ref,
    other_ref,
    left_ref,
    wo_ref,
    bias_ref,
    up_ref,
    down_ref,
    out_ref,
    mids,
):
    groups, rows, lanes = left_ref.shape
    width, near, _ = own_ref.shape
    core = place_ref[1]
    own = own_ref[...].reshape(width * near, rows)
    other = other_ref[...].reshape(width * near, rows)
    right = jnp.concatenate(
        [jnp.where(core == 0, own, other), jnp.where(core == 0, other, own)], axis=0
    )
    span = 2 * near
    cuts = lanes // COUPLING
    stacked = []
    for pair in range(groups // 2):
        left = jnp.concatenate([left_ref[2 * pair], left_ref[2 * pair + 1]], axis=1)
        outer = dot(right, left)
        low, high = outer[: width * near], outer[width * near :]
        for half in range(2):
            cut = slice(half * lanes, (half + 1) * lanes)
            pieces = [
                jnp.concatenate(
                    [low[e * near : (e + 1) * near, cut], high[e * near : (e + 1) * near, cut]],
                    axis=0,
                ).astype(BF16)
                for e in range(width)
            ]
            stacked.append(jnp.concatenate(pieces, axis=1))
    flat = jnp.concatenate(stacked, axis=0)
    projected = dot(flat, wo_ref[...])
    bias = bias_ref[...]
    channels = bias.shape[1]
    for g in range(groups):
        slot = place_ref[2 + g]
        for k in range(cuts):
            block = projected[g * span : (g + 1) * span, k * channels : (k + 1) * channels]
            scale = scale_ref[slot * cuts + k]
            mids[(g * cuts + k) * span : (g * cuts + k + 1) * span, :] = (
                pair_ref[slot * cuts + k].astype(F32) + (block + bias) * scale
            ).astype(BF16)
    middle = mids[...].astype(F32)
    normed = layer_norm(middle).astype(BF16)
    hidden = jnp.maximum(dot(normed, up_ref[...]), 0.0).astype(BF16)
    update = (middle + dot(hidden, down_ref[...])).astype(BF16)
    for g in range(groups):
        slot = place_ref[2 + g]
        for k in range(cuts):
            at = (g * cuts + k) * span
            out_ref[slot * cuts + k] = update[at : at + span]


def pair_block(place, pair, scale, own, other, left, wo, bias, up, down):
    span = 2 * own.shape[1]
    channels = pair.shape[2]

    def whole(a):
        return pl.BlockSpec(a.shape, lambda i, place, n=a.ndim: (0,) * n)

    tile = pl.BlockSpec((pair.shape[0], span, channels), lambda i, place: (0, place[0], 0))
    scale_tile = pl.BlockSpec((pair.shape[0], span, 1), lambda i, place: (0, place[0], 0))
    return pl.pallas_call(
        pair_kernel,
        grid_spec=pltpu.PrefetchScalarGridSpec(
            num_scalar_prefetch=1,
            grid=(1,),
            in_specs=[tile, scale_tile]
            + [whole(a) for a in (own, other, left, wo, bias, up, down)],
            out_specs=tile,
            scratch_shapes=[pltpu.VMEM((pair.shape[0] * span, channels), BF16)],
        ),
        out_shape=jax.ShapeDtypeStruct(pair.shape, pair.dtype),
        input_output_aliases={1: 0},
        compiler_params=pltpu.CompilerParams(
            dimension_semantics=("arbitrary",), vmem_limit_bytes=32 * 2**20
        ),
        cost_estimate=pl.CostEstimate(
            flops=3 * 10**9, bytes_accessed=6 * 2**20, transcendentals=0
        ),
    )(place, pair, scale, own, other, left, wo, bias, up, down)


def ring(size, shift):
    return [(i, (i + shift) % size) for i in range(size)]


def left_route(sizes):
    zs, ys, cs, xs, ls = sizes
    pairs = []
    place = lambda z, y, c, x, l: (((z * ys + y) * cs + c) * xs + x) * ls + l
    for z in range(zs):
        for y in range(ys):
            for c in range(cs):
                for x in range(xs):
                    for l in range(ls):
                        block = z // 2
                        slot = 4 * (z % 2) + 2 * c + y
                        pairs.append(
                            (
                                place(z, y, c, x, l),
                                place(x * ls + l, block // cs, block % cs, slot // ls, slot % ls),
                            )
                        )
    return pairs


def per_device(
    homolog_embedding,
    pair_features,
    row_present_mask,
    residue_keep_mask,
    query_weight,
    key_weight,
    content_matrix,
    sigmoid_switch_matrix,
    focus_merge_matrix,
    widening_matrix,
    narrowing_matrix,
    first_factor_matrix,
    second_factor_matrix,
    outer_product_weight,
    outer_product_bias,
    pair_up_weight,
    pair_down_weight,
):
    sizes = tuple(lax.axis_size(a) for a in SEQ + RES)
    zs, ys, cs, xs, ls = sizes
    z, yh, co, xi, li = (lax.axis_index(a) for a in SEQ + RES)
    span, breadth, channels = homolog_embedding.shape
    seq_count, res_count = zs * ys * cs, xs * ls
    owned = breadth // seq_count
    rows = span * seq_count
    pair_rows, _, pair_channels = pair_features.shape
    res_index = xi * ls + li
    seq_index = (z * ys + yh) * cs + co
    flags = row_present_mask.astype(F32)
    keep = residue_keep_mask.astype(F32)

    x = homolog_embedding.reshape(span, zs, cs, ys, owned, channels)
    x = x.transpose(1, 3, 2, 4, 0, 5).reshape(seq_count, owned, span, channels)
    x = lax.all_to_all(x, SEQ, split_axis=0, concat_axis=0, tiled=True)

    first = res_index * breadth + ((z * cs + co) * ys + yh) * owned
    mine = lax.dynamic_slice_in_dim(keep, first, owned, 0)
    keep_left = jnp.repeat(mine, COUPLING)[None, :]
    keep_right = jnp.tile(mine, COUPLING)[:, None]
    pad_left = jnp.zeros((owned, channels, owned, COUPLING), BF16)
    pad_right = jnp.zeros((owned, COUPLING, owned, channels), BF16)
    for k in range(owned):
        pad_left = pad_left.at[k, :, k].set(first_factor_matrix)
        pad_right = pad_right.at[k, :, k].set(second_factor_matrix.T)
    weights = (
        query_weight.T,
        key_weight,
        content_matrix.T,
        sigmoid_switch_matrix,
        focus_merge_matrix,
        widening_matrix,
        narrowing_matrix,
        pad_left.reshape(owned, channels, owned * COUPLING),
        pad_right.reshape(owned, COUPLING * owned, channels),
    )
    fill = ((flags - 1.0) * MASK_FILL)[:, None]
    update, left, right = columns(
        x, fill, flags[:, None], flags[None, :], keep_left, keep_right, weights
    )

    right = right.reshape(COUPLING, owned, rows)
    away = lax.ppermute(right, "yh", ring(ys, 1))
    right = jnp.where(
        yh == 0,
        jnp.concatenate([right, away], axis=1),
        jnp.concatenate([away, right], axis=1),
    )
    up = down = right
    blocks = [(0, right)]
    for k in range(1, zs // 2):
        up = lax.ppermute(up, "z", ring(zs, 1))
        down = lax.ppermute(down, "z", ring(zs, -1))
        blocks += [(-k, up), (k, down)]
    half = COUPLING // 2
    up = lax.ppermute(up[:half], "z", ring(zs, 1))
    down = lax.ppermute(down[half:], "z", ring(zs, -1))
    blocks.append((zs // 2, jnp.concatenate([up, down], axis=0)))
    blocks = [(k, own, lax.ppermute(own, "co", ring(cs, 1))) for k, own in blocks]

    left = lax.ppermute(left, SEQ + RES, left_route(sizes))
    near = jnp.stack([left, lax.ppermute(left, "yl", ring(ls, 1))])
    lower = lax.ppermute(near, "x", ring(xs, 1))
    upper = lax.ppermute(near, "x", ring(xs, -1))
    far = [
        lax.ppermute(lower[:1], "x", ring(xs, 1)),
        lax.ppermute(upper[1:], "x", ring(xs, -1)),
    ]
    left = jnp.concatenate([near, lower, upper] + far, axis=0)
    slots = []
    for shift in (0, -1, 1, 2):
        at = (xi + shift + xs) % xs
        slots += [at * ls + li, at * ls + 1 - li]
    slots = jnp.stack(slots)

    update = lax.all_to_all(update, SEQ, split_axis=0, concat_axis=0, tiled=True)
    update = update.reshape(zs, ys, cs, owned, span, channels).transpose(4, 0, 2, 1, 3, 5)
    update = update.reshape(span, breadth, channels)

    row_keep = lax.dynamic_slice_in_dim(keep, seq_index * pair_rows, pair_rows, 0)
    col_keep = lax.dynamic_slice_in_dim(keep, res_index * breadth, breadth, 0)
    norm = jnp.sum(flags) * row_keep[:, None] * col_keep[None, :]
    scale = (1.0 / jnp.maximum(norm, 1.0))[:, :, None]
    wo = outer_product_weight.reshape(COUPLING, COUPLING, pair_channels).transpose(1, 0, 2)
    wo = jnp.where(
        (jnp.arange(owned)[:, None] == jnp.arange(owned)[None, :])[None, :, None, :, None],
        wo[:, None, :, None, :],
        jnp.zeros((), BF16),
    ).reshape(COUPLING * owned * COUPLING, owned * pair_channels)
    pair = pair_features
    for k, own, other in blocks:
        at = (z + k + zs) % zs
        place = jnp.concatenate([jnp.stack([at, co]), slots]).astype(jnp.int32)
        pair = pair_block(
            place,
            pair,
            scale,
            own,
            other,
            left,
            wo,
            outer_product_bias[None, :],
            pair_up_weight,
            pair_down_weight,
        )
    return update, pair


def solution(mesh):
    grid = mesh.devices.reshape(8, 2, 2, 4, 2)
    fine = Mesh(grid, SEQ + RES)
    split = P(SEQ, RES, None)
    return jax.shard_map(
        per_device,
        mesh=fine,
        in_specs=(split, split) + (P(),) * 15,
        out_specs=(split, split),
        check_vma=False,
    )
```

```python
import functools
import math

import jax
import jax.numpy as jnp
from jax import lax
from jax.experimental import pallas as pl
from jax.experimental.pallas import tpu as pltpu
from jax.sharding import Mesh, PartitionSpec as P

HEADS = 8
HEAD = 32
COUPLING = 32
PARTS = 2
EARLY = 5
TIE = 2
EPSILON = 1e-05
MASK_FILL = 1000000000.0
SEQ = ("z", "yh", "co")
RES = ("x", "yl")
F32 = jnp.float32
BF16 = jnp.bfloat16


def layer_norm(values):
    centre = values - jnp.mean(values, axis=-1, keepdims=True)
    spread = jnp.mean(centre * centre, axis=-1, keepdims=True)
    return centre * lax.rsqrt(spread + EPSILON)


def dot(a, b):
    return jnp.dot(a, b, preferred_element_type=F32)


def dot_nt(a, b):
    return lax.dot_general(a, b, (((1,), (1,)), ((), ())), preferred_element_type=F32)


def column_kernel(
    x_ref,
    fill_ref,
    row_col_ref,
    row_row_ref,
    keep_left_ref,
    keep_right_ref,
    wq_ref,
    wk_ref,
    wv_ref,
    wg_ref,
    wm_ref,
    w1_ref,
    w2_ref,
    f1_ref,
    f2_ref,
    *refs,
):
    left_before, right_before = refs[:-6] if len(refs) > 6 else (None, None)
    out_ref, left_ref, right_ref, left_acc, right_acc, attended = refs[-6:]
    step = pl.program_id(0)
    shape = x_ref.shape
    rows = shape[0] * shape[2]
    x = x_ref[:, 0].reshape(rows, shape[3]).astype(F32)
    normed = layer_norm(x).astype(BF16)
    normed_t = normed.T
    queries_t = (dot(wq_ref[...], normed_t) * (1.0 / math.sqrt(HEAD))).astype(BF16)
    values_t = dot(wv_ref[...], normed_t).astype(BF16)
    keys = dot(normed, wk_ref[...]).astype(BF16)
    fill = fill_ref[...]
    ones = jnp.ones((16, rows), BF16)
    for h in range(HEADS):
        cut = slice(h * HEAD, (h + 1) * HEAD)
        scores = dot(keys[:, cut], queries_t[cut]) + fill
        peak = jnp.max(scores, axis=0, keepdims=True)
        weights = jnp.exp(scores - peak).astype(BF16)
        summed = dot(jnp.concatenate([values_t[cut], ones], axis=0), weights)
        attended[cut, :] = summed[:HEAD] / summed[HEAD : HEAD + 1]
    gate = jax.nn.sigmoid(dot(normed, wg_ref[...]))
    gated = (gate * attended[...].T).astype(BF16)
    after = (x + dot(gated, wm_ref[...])).astype(BF16)
    after_wide = after.astype(F32)
    normed = layer_norm(after_wide).astype(BF16)
    hidden = jnp.maximum(dot(normed, w1_ref[...]), 0.0).astype(BF16)
    update = (after_wide + dot(hidden, w2_ref[...])).astype(BF16)
    out_ref[:, 0] = update.reshape(shape[0], shape[2], shape[3])
    normed = layer_norm(update.astype(F32)).astype(BF16)
    left = dot(normed, f1_ref[0])
    right = dot_nt(f2_ref[0], normed)

    @pl.when(step == 0)
    def _():
        if left_before is None:
            left_acc[...] = left
            right_acc[...] = right
        else:
            left_acc[...] = left + left_before[...].astype(F32)
            right_acc[...] = right + right_before[...].astype(F32)

    @pl.when(step > 0)
    def _():
        left_acc[...] += left
        right_acc[...] += right

    @pl.when(step == pl.num_programs(0) - 1)
    def _():
        left_ref[...] = (left_acc[...] * row_col_ref[...] * keep_left_ref[...]).astype(BF16)
        right_ref[...] = (right_acc[...] * row_row_ref[...] * keep_right_ref[...]).astype(BF16)


def columns(x, fill, row_col, row_row, keep_left, keep_right, weights, first, count, before):
    sources, _, span, channels = x.shape
    rows = sources * span
    lanes = weights[-2].shape[2]

    def whole(a):
        return pl.BlockSpec(a.shape, lambda k, n=a.ndim: (0,) * n)

    def column(start):
        return pl.BlockSpec((sources, 1, span, channels), lambda k: (0, start + k, 0, 0))

    smalls = (fill, row_col, row_row, keep_left, keep_right)
    specs = [column(first)] + [whole(a) for a in smalls] + [whole(w) for w in weights[:-2]]
    specs += [pl.BlockSpec((1,) + w.shape[1:], lambda k: (first + k, 0, 0)) for w in weights[-2:]]
    specs += [whole(b) for b in before]
    return pl.pallas_call(
        column_kernel,
        grid=(count,),
        in_specs=specs,
        out_specs=(
            column(0),
            pl.BlockSpec((rows, lanes), lambda k: (0, 0)),
            pl.BlockSpec((lanes, rows), lambda k: (0, 0)),
        ),
        out_shape=(
            jax.ShapeDtypeStruct((sources, count, span, channels), BF16),
            jax.ShapeDtypeStruct((rows, lanes), BF16),
            jax.ShapeDtypeStruct((lanes, rows), BF16),
        ),
        scratch_shapes=[
            pltpu.VMEM((rows, lanes), F32),
            pltpu.VMEM((lanes, rows), F32),
            pltpu.VMEM((channels, rows), F32),
        ],
        compiler_params=pltpu.CompilerParams(
            dimension_semantics=("arbitrary",), vmem_limit_bytes=40 * 2**20
        ),
        cost_estimate=pl.CostEstimate(
            flops=6 * 10**9, bytes_accessed=4 * 2**20, transcendentals=4 * 10**6
        ),
    )(x, *smalls, *weights, *before)


def pair_kernel(
    place_ref,
    pair_ref,
    scale_ref,
    left_ref,
    wo_ref,
    bias_ref,
    up_ref,
    down_ref,
    *refs,
    count,
):
    blocks, (out_ref, rights, mids) = refs[: 2 * count], refs[-3:]
    step = pl.program_id(0)
    groups, rows, lanes = left_ref.shape
    width, near, _ = blocks[0].shape
    tall = width * near

    @pl.when(step == 0)
    def _():
        core = place_ref[count]
        for n in range(count):
            own = blocks[2 * n][...].reshape(tall, rows)
            other = blocks[2 * n + 1][...].reshape(tall, rows)
            rights[n, :tall] = jnp.where(core == 0, own, other)
            rights[n, tall:] = jnp.where(core == 0, other, own)

    right = rights[step]
    span = 2 * near
    cuts = lanes // COUPLING
    stacked = []
    for pair in range(groups // 2):
        left = jnp.concatenate([left_ref[2 * pair], left_ref[2 * pair + 1]], axis=1)
        outer = dot(right, left)
        low, high = outer[:tall], outer[tall:]
        for half in range(2):
            cut = slice(half * lanes, (half + 1) * lanes)
            pieces = [
                jnp.concatenate(
                    [low[e * near : (e + 1) * near, cut], high[e * near : (e + 1) * near, cut]],
                    axis=0,
                ).astype(BF16)
                for e in range(width)
            ]
            stacked.append(jnp.concatenate(pieces, axis=1))
    flat = jnp.concatenate(stacked, axis=0)
    projected = dot(flat, wo_ref[...])
    bias = bias_ref[...]
    channels = bias.shape[1]
    for g in range(groups):
        for k in range(cuts):
            i = g * cuts + k
            block = projected[g * span : (g + 1) * span, k * channels : (k + 1) * channels]
            mids[i * span : (i + 1) * span, :] = (
                pair_ref[i].astype(F32) + (block + bias) * scale_ref[i]
            ).astype(BF16)
    middle = mids[...].astype(F32)
    normed = layer_norm(middle).astype(BF16)
    hidden = jnp.maximum(dot(normed, up_ref[...]), 0.0).astype(BF16)
    update = (middle + dot(hidden, down_ref[...])).astype(BF16)
    out_ref[...] = update.reshape(out_ref.shape)


def pair_blocks(place, pair, scale, left, weights, blocks, before):
    count = len(blocks) // 2
    width, near, rows = blocks[0].shape
    span = 2 * near
    channels = pair.shape[2]

    def whole(a):
        return pl.BlockSpec(a.shape, lambda i, place, n=a.ndim: (0,) * n)

    tile = pl.BlockSpec((pair.shape[0], span, channels), lambda i, place: (0, place[i], 0))
    scale_tile = pl.BlockSpec((pair.shape[0], span, 1), lambda i, place: (0, place[i], 0))
    operands = [place, pair, scale, left, *weights, *blocks, *before]
    specs = [tile, scale_tile] + [whole(a) for a in (left, *weights, *blocks)]
    specs += [pl.BlockSpec(memory_space=pl.ANY) for _ in before]
    return pl.pallas_call(
        functools.partial(pair_kernel, count=count),
        grid_spec=pltpu.PrefetchScalarGridSpec(
            num_scalar_prefetch=1,
            grid=(count,),
            in_specs=specs,
            out_specs=tile,
            scratch_shapes=[
                pltpu.VMEM((count, 2 * width * near, rows), BF16),
                pltpu.VMEM((pair.shape[0] * span, channels), BF16),
            ],
        ),
        out_shape=jax.ShapeDtypeStruct(pair.shape, pair.dtype),
        input_output_aliases={len(operands) - 1: 0} if before else {},
        compiler_params=pltpu.CompilerParams(
            dimension_semantics=("arbitrary",), vmem_limit_bytes=40 * 2**20
        ),
        cost_estimate=pl.CostEstimate(
            flops=count * 2 * 10**9, bytes_accessed=6 * 2**20, transcendentals=0
        ),
    )(*operands)


def ring(size, shift):
    return [(i, (i + shift) % size) for i in range(size)]


def left_route(sizes):
    zs, ys, cs, xs, ls = sizes
    pairs = []
    place = lambda z, y, c, x, l: (((z * ys + y) * cs + c) * xs + x) * ls + l
    for z in range(zs):
        for y in range(ys):
            for c in range(cs):
                for x in range(xs):
                    for l in range(ls):
                        block = z // 2
                        slot = 4 * (z % 2) + 2 * c + y
                        pairs.append(
                            (
                                place(z, y, c, x, l),
                                place(x * ls + l, block // cs, block % cs, slot // ls, slot % ls),
                            )
                        )
    return pairs


def per_device(
    homolog_embedding,
    pair_features,
    row_present_mask,
    residue_keep_mask,
    query_weight,
    key_weight,
    content_matrix,
    sigmoid_switch_matrix,
    focus_merge_matrix,
    widening_matrix,
    narrowing_matrix,
    first_factor_matrix,
    second_factor_matrix,
    outer_product_weight,
    outer_product_bias,
    pair_up_weight,
    pair_down_weight,
):
    sizes = tuple(lax.axis_size(a) for a in SEQ + RES)
    zs, ys, cs, xs, ls = sizes
    z, yh, co, xi, li = (lax.axis_index(a) for a in SEQ + RES)
    span, breadth, channels = homolog_embedding.shape
    seq_count, res_count = zs * ys * cs, xs * ls
    owned = breadth // seq_count
    rows = span * seq_count
    pair_rows, _, pair_channels = pair_features.shape
    res_index = xi * ls + li
    seq_index = (z * ys + yh) * cs + co
    flags = row_present_mask.astype(F32)
    keep = residue_keep_mask.astype(F32)

    x = homolog_embedding.reshape(span, zs, cs, ys, owned, channels)
    x = x.transpose(1, 3, 2, 4, 0, 5).reshape(seq_count, owned, span, channels)
    x = lax.all_to_all(x, SEQ, split_axis=0, concat_axis=0, tiled=True)

    first = res_index * breadth + ((z * cs + co) * ys + yh) * owned
    mine = lax.dynamic_slice_in_dim(keep, first, owned, 0)
    keep_left = jnp.repeat(mine, COUPLING)[None, :]
    keep_right = jnp.tile(mine, COUPLING)[:, None]
    pad_left = jnp.zeros((owned, channels, owned, COUPLING), BF16)
    pad_right = jnp.zeros((owned, COUPLING, owned, channels), BF16)
    for k in range(owned):
        pad_left = pad_left.at[k, :, k].set(first_factor_matrix)
        pad_right = pad_right.at[k, :, k].set(second_factor_matrix.T)
    weights = (
        query_weight.T,
        key_weight,
        content_matrix.T,
        sigmoid_switch_matrix,
        focus_merge_matrix,
        widening_matrix,
        narrowing_matrix,
        pad_left.reshape(owned, channels, owned * COUPLING),
        pad_right.reshape(owned, COUPLING * owned, channels),
    )
    fill = ((flags - 1.0) * MASK_FILL)[:, None]
    updates, before = [], ()
    for n in range(PARTS):
        update, *before = columns(
            x,
            fill,
            flags[:, None],
            flags[None, :],
            keep_left,
            keep_right,
            weights,
            n * (owned // PARTS),
            owned // PARTS,
            before,
        )
        updates.append(update)
    left, right = before

    left = lax.ppermute(left, SEQ + RES, left_route(sizes))

    right = right.reshape(COUPLING, owned, rows)
    away = lax.ppermute(right, "yh", ring(ys, 1))
    right = jnp.where(
        yh == 0,
        jnp.concatenate([right, away], axis=1),
        jnp.concatenate([away, right], axis=1),
    )
    up = down = right
    blocks = [(0, right)]
    for k in range(1, zs // 2):
        if k == TIE:
            left, up, down = lax.optimization_barrier((left, up, down))
        up = lax.ppermute(up, "z", ring(zs, 1))
        down = lax.ppermute(down, "z", ring(zs, -1))
        blocks += [(-k, up), (k, down)]
    half = COUPLING // 2
    up = lax.ppermute(up[:half], "z", ring(zs, 1))
    down = lax.ppermute(down[half:], "z", ring(zs, -1))
    blocks.append((zs // 2, jnp.concatenate([up, down], axis=0)))
    blocks = [(k, own, lax.ppermute(own, "co", ring(cs, 1))) for k, own in blocks]

    sent = lax.all_to_all(updates[0], SEQ, split_axis=0, concat_axis=0, tiled=True)
    left, sent = lax.optimization_barrier((left, sent))
    left = jnp.broadcast_to(left[None], (res_count, *left.shape))
    left = lax.all_to_all(left, RES, split_axis=0, concat_axis=0, tiled=True)
    last, left = lax.optimization_barrier((updates[1], left))
    last = lax.all_to_all(last, SEQ, split_axis=0, concat_axis=0, tiled=True)
    updates = [sent, last]
    update = jnp.concatenate(updates, axis=1)
    update = update.reshape(zs, ys, cs, owned, span, channels).transpose(4, 0, 2, 1, 3, 5)
    update = update.reshape(span, breadth, channels)

    row_keep = lax.dynamic_slice_in_dim(keep, seq_index * pair_rows, pair_rows, 0)
    col_keep = lax.dynamic_slice_in_dim(keep, res_index * breadth, breadth, 0)
    norm = jnp.sum(flags) * row_keep[:, None] * col_keep[None, :]
    scale = (1.0 / jnp.maximum(norm, 1.0))[:, :, None]
    wo = outer_product_weight.reshape(COUPLING, COUPLING, pair_channels).transpose(1, 0, 2)
    wo = jnp.where(
        (jnp.arange(owned)[:, None] == jnp.arange(owned)[None, :])[None, :, None, :, None],
        wo[:, None, :, None, :],
        jnp.zeros((), BF16),
    ).reshape(COUPLING * owned * COUPLING, owned * pair_channels)
    pair_weights = (wo, outer_product_bias[None, :], pair_up_weight, pair_down_weight)
    before = ()
    for few in (blocks[:EARLY], blocks[EARLY:]):
        places = [(z + k + zs) % zs for k, _, _ in few] + [co]
        pair = pair_blocks(
            jnp.stack(places).astype(jnp.int32),
            pair_features,
            scale,
            left,
            pair_weights,
            [block for _, own, other in few for block in (own, other)],
            before,
        )
        before = (pair,)
    return update, pair


def solution(mesh):
    grid = mesh.devices.reshape(8, 2, 2, 4, 2)
    fine = Mesh(grid, SEQ + RES)
    split = P(SEQ, RES, None)
    return jax.shard_map(
        per_device,
        mesh=fine,
        in_specs=(split, split) + (P(),) * 15,
        out_specs=(split, split),
        check_vma=False,
    )
```

```python
import functools
import math

import jax
import jax.numpy as jnp
from jax import lax
from jax.experimental import pallas as pl
from jax.experimental.pallas import tpu as pltpu
from jax.sharding import Mesh, PartitionSpec as P

HEADS = 8
HEAD = 32
COUPLING = 32
PARTS = 2
EARLY = 5
TIE = 1
EPSILON = 1e-05
MASK_FILL = 1000000000.0
SEQ = ("z", "yh", "co")
RES = ("x", "yl")
F32 = jnp.float32
BF16 = jnp.bfloat16


def layer_norm(values):
    centre = values - jnp.mean(values, axis=-1, keepdims=True)
    spread = jnp.mean(centre * centre, axis=-1, keepdims=True)
    return centre * lax.rsqrt(spread + EPSILON)


def dot(a, b):
    return jnp.dot(a, b, preferred_element_type=F32)


def dot_nt(a, b):
    return lax.dot_general(a, b, (((1,), (1,)), ((), ())), preferred_element_type=F32)


def column_kernel(
    x_ref,
    fill_ref,
    row_col_ref,
    row_row_ref,
    keep_left_ref,
    keep_right_ref,
    wq_ref,
    wk_ref,
    wv_ref,
    wg_ref,
    wm_ref,
    w1_ref,
    w2_ref,
    f1_ref,
    f2_ref,
    *refs,
):
    left_before, right_before = refs[:-4] if len(refs) > 4 else (None, None)
    out_ref, left_ref, right_ref, attended = refs[-4:]
    sources, count, span, channels = x_ref.shape
    rows = sources * span
    tall = count * rows
    x = jnp.concatenate(
        [x_ref[:, c].reshape(rows, channels) for c in range(count)], axis=0
    ).astype(F32)
    normed = layer_norm(x).astype(BF16)
    normed_t = normed.T
    queries_t = (dot(wq_ref[...], normed_t) * (1.0 / math.sqrt(HEAD))).astype(BF16)
    values_t = dot(wv_ref[...], normed_t).astype(BF16)
    keys = dot(normed, wk_ref[...]).astype(BF16)
    fill = fill_ref[...]
    ones = jnp.ones((16, rows), BF16)
    for h in range(HEADS):
        for c in range(count):
            cut = slice(h * HEAD, (h + 1) * HEAD)
            col = slice(c * rows, (c + 1) * rows)
            scores = dot(keys[col, cut], queries_t[cut, col]) + fill
            peak = jnp.max(scores, axis=0, keepdims=True)
            weights = jnp.exp(scores - peak)
            total = jnp.sum(weights, axis=0, keepdims=True)
            summed = dot(values_t[cut, col], weights.astype(BF16))
            attended[cut, col] = summed / total
    gate = jax.nn.sigmoid(dot(normed, wg_ref[...]))
    gated = (gate * attended[...].T).astype(BF16)
    after = (x + dot(gated, wm_ref[...])).astype(BF16)
    after_wide = after.astype(F32)
    normed = layer_norm(after_wide).astype(BF16)
    hidden = jnp.maximum(dot(normed, w1_ref[...]), 0.0).astype(BF16)
    update = (after_wide + dot(hidden, w2_ref[...])).astype(BF16)
    for c in range(count):
        out_ref[:, c] = update[c * rows : (c + 1) * rows].reshape(sources, span, channels)
    normed = layer_norm(update.astype(F32)).astype(BF16)
    left = sum(dot(normed[c * rows : (c + 1) * rows], f1_ref[c]) for c in range(count))
    right = sum(dot_nt(f2_ref[c], normed[c * rows : (c + 1) * rows]) for c in range(count))
    left = (left * row_col_ref[...] * keep_left_ref[...]).astype(BF16)
    right = (right * row_row_ref[...] * keep_right_ref[...]).astype(BF16)
    if left_before is not None:
        left += left_before[...]
        right += right_before[...]
    left_ref[...] = left
    right_ref[...] = right


def columns(x, fill, row_col, row_row, keep_left, keep_right, weights, first, count, before):
    sources, _, span, channels = x.shape
    rows = sources * span
    lanes = weights[-2].shape[2]

    def whole(a):
        return pl.BlockSpec(a.shape, lambda k, n=a.ndim: (0,) * n)

    def column(start):
        return pl.BlockSpec((sources, count, span, channels), lambda k: (0, start, 0, 0))

    smalls = (fill, row_col, row_row, keep_left, keep_right)
    specs = [column(first // count)] + [whole(a) for a in smalls] + [whole(w) for w in weights[:-2]]
    specs += [pl.BlockSpec((count,) + w.shape[1:], lambda k: (first // count, 0, 0)) for w in weights[-2:]]
    specs += [whole(b) for b in before]
    return pl.pallas_call(
        column_kernel,
        grid=(1,),
        in_specs=specs,
        out_specs=(
            column(0),
            pl.BlockSpec((rows, lanes), lambda k: (0, 0)),
            pl.BlockSpec((lanes, rows), lambda k: (0, 0)),
        ),
        out_shape=(
            jax.ShapeDtypeStruct((sources, count, span, channels), BF16),
            jax.ShapeDtypeStruct((rows, lanes), BF16),
            jax.ShapeDtypeStruct((lanes, rows), BF16),
        ),
        scratch_shapes=[
            pltpu.VMEM((channels, count * rows), F32),
        ],
        compiler_params=pltpu.CompilerParams(
            dimension_semantics=("arbitrary",), vmem_limit_bytes=28 * 2**20
        ),
        cost_estimate=pl.CostEstimate(
            flops=6 * 10**9, bytes_accessed=4 * 2**20, transcendentals=4 * 10**6
        ),
    )(x, *smalls, *weights, *before)


def pair_kernel(
    place_ref,
    pair_ref,
    scale_ref,
    left_ref,
    wo_ref,
    bias_ref,
    up_ref,
    down_ref,
    *refs,
    count,
):
    blocks, (out_ref, flats) = refs[: 2 * count], refs[-2:]
    groups, rows, lanes = left_ref.shape
    width, near, _ = blocks[0].shape
    tall = width * near
    span = 2 * near
    cuts = lanes // COUPLING
    many = groups * span
    core = place_ref[count]
    for n in range(count):
        own = blocks[2 * n][...].reshape(tall, rows)
        other = blocks[2 * n + 1][...].reshape(tall, rows)
        right = jnp.concatenate(
            [jnp.where(core == 0, own, other), jnp.where(core == 0, other, own)], axis=0
        )
        for pair in range(groups // 2):
            left = jnp.concatenate([left_ref[2 * pair], left_ref[2 * pair + 1]], axis=1)
            outer = dot(right, left)
            low, high = outer[:tall], outer[tall:]
            for half in range(2):
                cut = slice(half * lanes, (half + 1) * lanes)
                at = n * many + (2 * pair + half) * span
                for e in range(width):
                    part = slice(e * near, (e + 1) * near)
                    flats[at : at + span, e * lanes : (e + 1) * lanes] = jnp.concatenate(
                        [low[part, cut], high[part, cut]], axis=0
                    ).astype(BF16)
    projected = dot(flats[...], wo_ref[...])
    bias = bias_ref[...]
    channels = bias.shape[1]
    if len(refs) > 2 * count + 2:
        out_ref[...] = refs[2 * count][...]
    for n in range(count):
        spot = pl.ds(pl.multiple_of(place_ref[n] * span, span), span)
        kept = jnp.broadcast_to(scale_ref[spot, :], (span, channels))
        middle = []
        for g in range(groups):
            for k in range(cuts):
                i = g * cuts + k
                at = n * many + g * span
                block = projected[at : at + span, k * channels : (k + 1) * channels]
                scale = jnp.where(place_ref[count + 1 + i] > 0, kept, 1.0)
                middle.append(
                    (pair_ref[i, spot, :].astype(F32) + (block + bias) * scale).astype(BF16)
                )
        middle = jnp.concatenate(middle, axis=0).astype(F32)
        normed = layer_norm(middle).astype(BF16)
        hidden = jnp.maximum(dot(normed, up_ref[...]), 0.0).astype(BF16)
        update = (middle + dot(hidden, down_ref[...])).astype(BF16)
        out_ref[:, spot, :] = update.reshape(groups * cuts, span, channels)


def pair_blocks(place, pair, scale, left, weights, blocks, before):
    count = len(blocks) // 2
    _, near, rows = blocks[0].shape
    groups, _, lanes = left.shape

    def whole(a):
        return pl.BlockSpec(a.shape, lambda i, place, n=a.ndim: (0,) * n)

    operands = [pair, scale, left, *weights, *blocks, *before]
    return pl.pallas_call(
        functools.partial(pair_kernel, count=count),
        grid_spec=pltpu.PrefetchScalarGridSpec(
            num_scalar_prefetch=1,
            grid=(1,),
            in_specs=[whole(a) for a in operands],
            out_specs=whole(pair),
            scratch_shapes=[
                pltpu.VMEM((count * groups * 2 * near, COUPLING * lanes), BF16),
            ],
        ),
        out_shape=jax.ShapeDtypeStruct(pair.shape, pair.dtype),
        compiler_params=pltpu.CompilerParams(
            dimension_semantics=("arbitrary",), vmem_limit_bytes=36 * 2**20
        ),
        cost_estimate=pl.CostEstimate(
            flops=count * 2 * 10**9, bytes_accessed=6 * 2**20, transcendentals=0
        ),
    )(place, *operands)


NEWPAIR = True


def ring(size, shift):
    return [(i, (i + shift) % size) for i in range(size)]


def left_route(sizes):
    zs, ys, cs, xs, ls = sizes
    pairs = []
    place = lambda z, y, c, x, l: (((z * ys + y) * cs + c) * xs + x) * ls + l
    for z in range(zs):
        for y in range(ys):
            for c in range(cs):
                for x in range(xs):
                    for l in range(ls):
                        block = z // 2
                        slot = 4 * (z % 2) + 2 * c + y
                        pairs.append(
                            (
                                place(z, y, c, x, l),
                                place(x * ls + l, block // cs, block % cs, slot // ls, slot % ls),
                            )
                        )
    return pairs


def per_device(
    homolog_embedding,
    pair_features,
    row_present_mask,
    residue_keep_mask,
    query_weight,
    key_weight,
    content_matrix,
    sigmoid_switch_matrix,
    focus_merge_matrix,
    widening_matrix,
    narrowing_matrix,
    first_factor_matrix,
    second_factor_matrix,
    outer_product_weight,
    outer_product_bias,
    pair_up_weight,
    pair_down_weight,
):
    sizes = tuple(lax.axis_size(a) for a in SEQ + RES)
    zs, ys, cs, xs, ls = sizes
    z, yh, co, xi, li = (lax.axis_index(a) for a in SEQ + RES)
    span, breadth, channels = homolog_embedding.shape
    seq_count, res_count = zs * ys * cs, xs * ls
    owned = breadth // seq_count
    rows = span * seq_count
    pair_rows, _, pair_channels = pair_features.shape
    res_index = xi * ls + li
    seq_index = (z * ys + yh) * cs + co
    flags = row_present_mask.astype(F32)
    keep = residue_keep_mask.astype(F32)

    x = homolog_embedding.reshape(span, zs, cs, ys, owned, channels)
    x = x.transpose(1, 3, 2, 4, 0, 5).reshape(seq_count, owned, span, channels)
    x = lax.all_to_all(x, SEQ, split_axis=0, concat_axis=0, tiled=True)

    row_keep = lax.dynamic_slice_in_dim(
        residue_keep_mask, seq_index * pair_rows, pair_rows, 0
    )
    col_keep = lax.dynamic_slice_in_dim(keep, res_index * breadth, breadth, 0)
    scale = (1.0 / jnp.maximum(jnp.sum(flags) * col_keep, 1.0))[:, None]
    wo = outer_product_weight.reshape(COUPLING, COUPLING, pair_channels).transpose(1, 0, 2)
    wo = jnp.where(
        (jnp.arange(owned)[:, None] == jnp.arange(owned)[None, :])[None, :, None, :, None],
        wo[:, None, :, None, :],
        jnp.zeros((), BF16),
    ).reshape(COUPLING * owned * COUPLING, owned * pair_channels)
    steps = (0, *(s * k for k in range(1, zs // 2) for s in (-1, 1)), zs // 2)
    places = jnp.stack([(z + k + zs) % zs for k in steps])
    places = [
        jnp.concatenate([part, co[None], row_keep]).astype(jnp.int32)
        for part in (places[:EARLY], places[EARLY:])
    ]
    x, wo, scale, places = lax.optimization_barrier((x, wo, scale, places))

    first = res_index * breadth + ((z * cs + co) * ys + yh) * owned
    mine = lax.dynamic_slice_in_dim(keep, first, owned, 0)
    keep_left = jnp.repeat(mine, COUPLING)[None, :]
    keep_right = jnp.tile(mine, COUPLING)[:, None]
    pad_left = jnp.zeros((owned, channels, owned, COUPLING), BF16)
    pad_right = jnp.zeros((owned, COUPLING, owned, channels), BF16)
    for k in range(owned):
        pad_left = pad_left.at[k, :, k].set(first_factor_matrix)
        pad_right = pad_right.at[k, :, k].set(second_factor_matrix.T)
    weights = (
        query_weight.T,
        key_weight,
        content_matrix.T,
        sigmoid_switch_matrix,
        focus_merge_matrix,
        widening_matrix,
        narrowing_matrix,
        pad_left.reshape(owned, channels, owned * COUPLING),
        pad_right.reshape(owned, COUPLING * owned, channels),
    )
    fill = ((flags - 1.0) * MASK_FILL)[:, None]
    updates, before = [], ()
    for n in range(PARTS):
        update, *before = columns(
            x,
            fill,
            flags[:, None],
            flags[None, :],
            keep_left,
            keep_right,
            weights,
            n * (owned // PARTS),
            owned // PARTS,
            before,
        )
        updates.append(update)
    left, right = before

    left = lax.ppermute(left, SEQ + RES, left_route(sizes))

    right = right.reshape(COUPLING, owned, rows)
    away = lax.ppermute(right, "yh", ring(ys, 1))
    right = jnp.where(
        yh == 0,
        jnp.concatenate([right, away], axis=1),
        jnp.concatenate([away, right], axis=1),
    )
    up = down = right
    blocks = [right]
    for k in range(1, zs // 2):
        if k == TIE:
            left, up, down = lax.optimization_barrier((left, up, down))
        up = lax.ppermute(up, "z", ring(zs, 1))
        down = lax.ppermute(down, "z", ring(zs, -1))
        blocks += [up, down]
    half = COUPLING // 2
    up = lax.ppermute(up[:half], "z", ring(zs, 1))
    down = lax.ppermute(down[half:], "z", ring(zs, -1))
    blocks.append(jnp.concatenate([up, down], axis=0))
    blocks = [(own, lax.ppermute(own, "co", ring(cs, 1))) for own in blocks]

    sent = lax.all_to_all(updates[0], SEQ, split_axis=0, concat_axis=0, tiled=True)
    left, sent = lax.optimization_barrier((left, sent))
    left = jnp.broadcast_to(left[None], (res_count, *left.shape))
    left = lax.all_to_all(left, RES, split_axis=0, concat_axis=0, tiled=True)
    last, left = lax.optimization_barrier((updates[1], left))
    last = lax.all_to_all(last, SEQ, split_axis=0, concat_axis=0, tiled=True)
    updates = [sent, last]
    update = jnp.concatenate(updates, axis=1)
    update = update.reshape(zs, ys, cs, owned, span, channels).transpose(4, 0, 2, 1, 3, 5)
    update = update.reshape(span, breadth, channels)

    pair_weights = (wo, outer_product_bias[None, :], pair_up_weight, pair_down_weight)
    before = ()
    for place, few in zip(places, (blocks[:EARLY], blocks[EARLY:])):
        pair = pair_blocks(
            place,
            pair_features,
            scale,
            left,
            pair_weights,
            [block for own, other in few for block in (own, other)],
            before,
        )
        before = (pair,)
    return update, pair


def solution(mesh):
    grid = mesh.devices.reshape(8, 2, 2, 4, 2)
    fine = Mesh(grid, SEQ + RES)
    split = P(SEQ, RES, None)
    return jax.shard_map(
        per_device,
        mesh=fine,
        in_specs=(split, split) + (P(),) * 15,
        out_specs=(split, split),
        check_vma=False,
    )
```

```python
import functools
import math

import jax
import jax.numpy as jnp
from jax import lax
from jax.experimental import pallas as pl
from jax.experimental.pallas import tpu as pltpu
from jax.sharding import Mesh, PartitionSpec as P

HEADS = 8
HEAD = 32
COUPLING = 32
PARTS = 2
EARLY = 7
EPSILON = 1e-05
MASK_FILL = 1000000000.0
SEQ = ("z", "yh", "co")
RES = ("x", "yl")
F32 = jnp.float32
BF16 = jnp.bfloat16


def layer_norm(values):
    centre = values - jnp.mean(values, axis=-1, keepdims=True)
    spread = jnp.mean(centre * centre, axis=-1, keepdims=True)
    return centre * lax.rsqrt(spread + EPSILON)


def dot(a, b):
    return jnp.dot(a, b, preferred_element_type=F32)


def dot_nt(a, b):
    return lax.dot_general(a, b, (((1,), (1,)), ((), ())), preferred_element_type=F32)


def column_kernel(
    x_ref,
    fill_ref,
    row_col_ref,
    row_row_ref,
    keep_left_ref,
    keep_right_ref,
    wq_ref,
    wk_ref,
    wv_ref,
    wg_ref,
    wm_ref,
    w1_ref,
    w2_ref,
    f1_ref,
    f2_ref,
    out_ref,
    left_ref,
    right_ref,
    attended,
):
    sources, count, span, channels = x_ref.shape
    rows = sources * span
    tall = count * rows
    x = jnp.concatenate(
        [x_ref[:, c].reshape(rows, channels) for c in range(count)], axis=0
    ).astype(F32)
    normed = layer_norm(x).astype(BF16)
    normed_t = normed.T
    queries_t = (dot(wq_ref[...], normed_t) * (1.0 / math.sqrt(HEAD))).astype(BF16)
    values_t = dot(wv_ref[...], normed_t).astype(BF16)
    keys = dot(normed, wk_ref[...]).astype(BF16)
    fill = fill_ref[...]
    ones = jnp.ones((16, rows), BF16)
    for h in range(HEADS):
        for c in range(count):
            cut = slice(h * HEAD, (h + 1) * HEAD)
            col = slice(c * rows, (c + 1) * rows)
            scores = dot(keys[col, cut], queries_t[cut, col]) + fill
            peak = jnp.max(scores, axis=0, keepdims=True)
            weights = jnp.exp(scores - peak)
            total = jnp.sum(weights, axis=0, keepdims=True)
            summed = dot(values_t[cut, col], weights.astype(BF16))
            attended[cut, col] = summed / total
    gate = jax.nn.sigmoid(dot(normed, wg_ref[...]))
    gated = (gate * attended[...].T).astype(BF16)
    after = (x + dot(gated, wm_ref[...])).astype(BF16)
    after_wide = after.astype(F32)
    normed = layer_norm(after_wide).astype(BF16)
    hidden = jnp.maximum(dot(normed, w1_ref[...]), 0.0).astype(BF16)
    update = (after_wide + dot(hidden, w2_ref[...])).astype(BF16)
    for c in range(count):
        out_ref[:, c] = update[c * rows : (c + 1) * rows].reshape(sources, span, channels)
    normed = layer_norm(update.astype(F32)).astype(BF16)
    left = sum(dot(normed[c * rows : (c + 1) * rows], f1_ref[c]) for c in range(count))
    right = sum(dot_nt(f2_ref[c], normed[c * rows : (c + 1) * rows]) for c in range(count))
    left_ref[...] = (left * row_col_ref[...] * keep_left_ref[...]).astype(BF16)
    right_ref[...] = (right * row_row_ref[...] * keep_right_ref[...]).astype(BF16)


def columns(x, fill, row_col, row_row, keep_left, keep_right, weights, first, count):
    sources, _, span, channels = x.shape
    rows = sources * span
    lanes = weights[-2].shape[2]

    def whole(a):
        return pl.BlockSpec(a.shape, lambda k, n=a.ndim: (0,) * n)

    def column(start):
        return pl.BlockSpec((sources, count, span, channels), lambda k: (0, start, 0, 0))

    smalls = (fill, row_col, row_row, keep_left, keep_right)
    specs = [column(first // count)] + [whole(a) for a in smalls] + [whole(w) for w in weights[:-2]]
    specs += [pl.BlockSpec((count,) + w.shape[1:], lambda k: (first // count, 0, 0)) for w in weights[-2:]]
    return pl.pallas_call(
        column_kernel,
        grid=(1,),
        in_specs=specs,
        out_specs=(
            column(0),
            pl.BlockSpec((rows, lanes), lambda k: (0, 0)),
            pl.BlockSpec((lanes, rows), lambda k: (0, 0)),
        ),
        out_shape=(
            jax.ShapeDtypeStruct((sources, count, span, channels), BF16),
            jax.ShapeDtypeStruct((rows, lanes), BF16),
            jax.ShapeDtypeStruct((lanes, rows), BF16),
        ),
        scratch_shapes=[
            pltpu.VMEM((channels, count * rows), F32),
        ],
        compiler_params=pltpu.CompilerParams(
            dimension_semantics=("arbitrary",), vmem_limit_bytes=28 * 2**20
        ),
        cost_estimate=pl.CostEstimate(
            flops=6 * 10**9, bytes_accessed=4 * 2**20, transcendentals=4 * 10**6
        ),
    )(x, *smalls, *weights)


def pair_kernel(
    place_ref,
    pair_ref,
    scale_ref,
    left_ref,
    wo_ref,
    bias_ref,
    up_ref,
    down_ref,
    *refs,
    count,
):
    blocks, (out_ref, flats) = refs[:count], refs[-2:]
    groups, rows, lanes = left_ref.shape
    width, span, _ = blocks[0].shape
    cuts = lanes // COUPLING
    many = groups * span
    for n in range(count):
        right = blocks[n][...].reshape(width * span, rows)
        for pair in range(groups // 2):
            left = jnp.concatenate([left_ref[2 * pair], left_ref[2 * pair + 1]], axis=1)
            outer = dot(right, left).astype(BF16)
            for half in range(2):
                cut = slice(half * lanes, (half + 1) * lanes)
                at = n * many + (2 * pair + half) * span
                for e in range(width):
                    flats[at : at + span, e * lanes : (e + 1) * lanes] = outer[
                        e * span : (e + 1) * span, cut
                    ]
    projected = dot(flats[...], wo_ref[...])
    bias = bias_ref[...]
    channels = bias.shape[1]
    if len(refs) > count + 2:
        out_ref[...] = refs[count][...]
    for n in range(count):
        spot = pl.ds(pl.multiple_of(place_ref[n] * span, span), span)
        kept = jnp.broadcast_to(scale_ref[spot, :], (span, channels))
        middle = []
        for g in range(groups):
            for k in range(cuts):
                i = g * cuts + k
                at = n * many + g * span
                block = projected[at : at + span, k * channels : (k + 1) * channels]
                scale = jnp.where(place_ref[count + i] > 0, kept, 1.0)
                middle.append(
                    (pair_ref[i, spot, :].astype(F32) + (block + bias) * scale).astype(BF16)
                )
        middle = jnp.concatenate(middle, axis=0).astype(F32)
        normed = layer_norm(middle).astype(BF16)
        hidden = jnp.maximum(dot(normed, up_ref[...]), 0.0).astype(BF16)
        update = (middle + dot(hidden, down_ref[...])).astype(BF16)
        out_ref[:, spot, :] = update.reshape(groups * cuts, span, channels)


def pair_blocks(place, pair, scale, left, weights, blocks, before):
    count = len(blocks)
    _, span, rows = blocks[0].shape
    groups, _, lanes = left.shape

    def whole(a):
        return pl.BlockSpec(a.shape, lambda i, place, n=a.ndim: (0,) * n)

    operands = [pair, scale, left, *weights, *blocks, *before]
    return pl.pallas_call(
        functools.partial(pair_kernel, count=count),
        grid_spec=pltpu.PrefetchScalarGridSpec(
            num_scalar_prefetch=1,
            grid=(1,),
            in_specs=[whole(a) for a in operands],
            out_specs=whole(pair),
            scratch_shapes=[
                pltpu.VMEM((count * groups * span, COUPLING * lanes), BF16),
            ],
        ),
        out_shape=jax.ShapeDtypeStruct(pair.shape, pair.dtype),
        compiler_params=pltpu.CompilerParams(
            dimension_semantics=("arbitrary",), vmem_limit_bytes=36 * 2**20
        ),
        cost_estimate=pl.CostEstimate(
            flops=count * 2 * 10**9, bytes_accessed=6 * 2**20, transcendentals=0
        ),
    )(place, *operands)


NEWPAIR = True


def ring(size, shift):
    return [(i, (i + shift) % size) for i in range(size)]


def left_route(sizes):
    zs, ys, cs, xs, ls = sizes
    pairs = []
    place = lambda z, y, c, x, l: (((z * ys + y) * cs + c) * xs + x) * ls + l
    for z in range(zs):
        for y in range(ys):
            for c in range(cs):
                for x in range(xs):
                    for l in range(ls):
                        block = z // 2
                        slot = 4 * (z % 2) + 2 * y + c
                        pairs.append(
                            (
                                place(z, y, c, x, l),
                                place(x * ls + l, block // cs, block % cs, slot // ls, slot % ls),
                            )
                        )
    return pairs


def per_device(
    homolog_embedding,
    pair_features,
    row_present_mask,
    residue_keep_mask,
    query_weight,
    key_weight,
    content_matrix,
    sigmoid_switch_matrix,
    focus_merge_matrix,
    widening_matrix,
    narrowing_matrix,
    first_factor_matrix,
    second_factor_matrix,
    outer_product_weight,
    outer_product_bias,
    pair_up_weight,
    pair_down_weight,
):
    sizes = tuple(lax.axis_size(a) for a in SEQ + RES)
    zs, ys, cs, xs, ls = sizes
    z, yh, co, xi, li = (lax.axis_index(a) for a in SEQ + RES)
    span, breadth, channels = homolog_embedding.shape
    seq_count, res_count = zs * ys * cs, xs * ls
    owned = breadth // seq_count
    rows = span * seq_count
    pair_rows, _, pair_channels = pair_features.shape
    res_index = xi * ls + li
    seq_index = (z * ys + yh) * cs + co
    flags = row_present_mask.astype(F32)
    keep = residue_keep_mask.astype(F32)

    x = homolog_embedding.transpose(1, 0, 2).reshape(seq_count, owned, span, channels)
    x = lax.all_to_all(x, SEQ, split_axis=0, concat_axis=0, tiled=True)

    row_keep = lax.dynamic_slice_in_dim(
        residue_keep_mask, seq_index * pair_rows, pair_rows, 0
    )
    col_keep = lax.dynamic_slice_in_dim(keep, res_index * breadth, breadth, 0)
    scale = (1.0 / jnp.maximum(jnp.sum(flags) * col_keep, 1.0))[:, None]
    wo = outer_product_weight.reshape(COUPLING, COUPLING, pair_channels).transpose(1, 0, 2)
    wo = jnp.where(
        (jnp.arange(owned)[:, None] == jnp.arange(owned)[None, :])[None, :, None, :, None],
        wo[:, None, :, None, :],
        jnp.zeros((), BF16),
    ).reshape(COUPLING * owned * COUPLING, owned * pair_channels)
    way = 1 - 2 * co
    steps = [jnp.zeros_like(z)]
    for k in range(1, zs // 2):
        steps += [-k * way, k * way]
    places = jnp.stack([(z + k + zs) % zs for k in steps + [zs // 2]])
    places = [
        jnp.concatenate([part, row_keep]).astype(jnp.int32)
        for part in (places[:EARLY], places[EARLY:])
    ]
    x, wo, scale, places = lax.optimization_barrier((x, wo, scale, places))

    first = res_index * breadth + seq_index * owned
    mine = lax.dynamic_slice_in_dim(keep, first, owned, 0)
    keep_left = jnp.repeat(mine, COUPLING)[None, :]
    keep_right = jnp.tile(mine, COUPLING)[:, None]
    pad_left = jnp.zeros((owned, channels, owned, COUPLING), BF16)
    pad_right = jnp.zeros((owned, COUPLING, owned, channels), BF16)
    for k in range(owned):
        pad_left = pad_left.at[k, :, k].set(first_factor_matrix)
        pad_right = pad_right.at[k, :, k].set(second_factor_matrix.T)
    weights = (
        query_weight.T,
        key_weight,
        content_matrix.T,
        sigmoid_switch_matrix,
        focus_merge_matrix,
        widening_matrix,
        narrowing_matrix,
        pad_left.reshape(owned, channels, owned * COUPLING),
        pad_right.reshape(owned, COUPLING * owned, channels),
    )
    fill = ((flags - 1.0) * MASK_FILL)[:, None]
    updates, lefts, rights = [], [], []
    for n in range(PARTS):
        update, left, right = columns(
            x,
            fill,
            flags[:, None],
            flags[None, :],
            keep_left,
            keep_right,
            weights,
            n * (owned // PARTS),
            owned // PARTS,
        )
        updates.append(update)
        lefts.append(left)
        rights.append(right)
    left, right = sum(lefts), sum(rights)

    left = lax.ppermute(left, SEQ + RES, left_route(sizes))

    sent = lax.all_to_all(updates[0], SEQ, split_axis=0, concat_axis=0, tiled=True)
    right, sent = lax.optimization_barrier((right, sent))
    right = right.reshape(COUPLING, owned, rows)
    away = lax.ppermute(right, "yh", ring(ys, 1))
    mine = jnp.stack([jnp.where(yh == 0, right, away), jnp.where(yh == 0, away, right)])
    left, mine = lax.optimization_barrier((left, mine))
    away = lax.ppermute(mine, "co", ring(cs, 1))
    right = jnp.stack(
        [jnp.where(co == 0, mine, away), jnp.where(co == 0, away, mine)], axis=1
    )
    right = right.transpose(2, 0, 1, 3, 4).reshape(COUPLING, ys * cs * owned, rows)
    turn = [
        (n * cs + c, (n + (1 if c == 0 else -1)) % zs * cs + c) for n in range(zs) for c in range(cs)
    ]
    blocks = [right]
    send = right
    for k in range(1, zs // 2):
        send = lax.ppermute(send, ("z", "co"), turn)
        blocks += [send, lax.ppermute(send, "co", ring(cs, 1))]
    half = COUPLING // 2
    send = lax.dynamic_slice_in_dim(send, co * half, half, 0)

    left = jnp.broadcast_to(left[None], (res_count, *left.shape))
    left = lax.all_to_all(left, RES, split_axis=0, concat_axis=0, tiled=True)
    left, send = lax.optimization_barrier((left, send))
    send = lax.ppermute(send, ("z", "co"), turn)
    away = lax.ppermute(send, "co", ring(cs, 1))
    blocks.append(
        jnp.concatenate([jnp.where(co == 0, send, away), jnp.where(co == 0, away, send)], axis=0)
    )
    last, left = lax.optimization_barrier((updates[1], left))
    last = lax.all_to_all(last, SEQ, split_axis=0, concat_axis=0, tiled=True)
    updates = [sent, last]
    update = jnp.concatenate(updates, axis=1).reshape(breadth, span, channels).transpose(1, 0, 2)

    pair_weights = (wo, outer_product_bias[None, :], pair_up_weight, pair_down_weight)
    before = ()
    for place, few in zip(places, (blocks[:EARLY], blocks[EARLY:])):
        pair = pair_blocks(
            place,
            pair_features,
            scale,
            left,
            pair_weights,
            few,
            before,
        )
        before = (pair,)
    return update, pair


def solution(mesh):
    grid = mesh.devices.reshape(8, 2, 2, 4, 2)
    fine = Mesh(grid, SEQ + RES)
    split = P(SEQ, RES, None)
    return jax.shard_map(
        per_device,
        mesh=fine,
        in_specs=(split, split) + (P(),) * 15,
        out_specs=(split, split),
        check_vma=False,
    )
```

```python
import functools
import math

import jax
import jax.numpy as jnp
from jax import lax
from jax.experimental import pallas as pl
from jax.experimental.pallas import tpu as pltpu
from jax.sharding import Mesh, PartitionSpec as P

HEADS = 8
HEAD = 32
COUPLING = 32
PARTS = 2
EARLY = 5
TIE = 1
EPSILON = 1e-05
MASK_FILL = 1000000000.0
SEQ = ("z", "yh", "co")
RES = ("x", "yl")
F32 = jnp.float32
BF16 = jnp.bfloat16


def layer_norm(values):
    centre = values - jnp.mean(values, axis=-1, keepdims=True)
    spread = jnp.mean(centre * centre, axis=-1, keepdims=True)
    return centre * lax.rsqrt(spread + EPSILON)


def dot(a, b):
    return jnp.dot(a, b, preferred_element_type=F32)


def dot_nt(a, b):
    return lax.dot_general(a, b, (((1,), (1,)), ((), ())), preferred_element_type=F32)


def column_kernel(
    x_ref,
    fill_ref,
    row_col_ref,
    row_row_ref,
    keep_left_ref,
    keep_right_ref,
    wq_ref,
    wk_ref,
    wv_ref,
    wg_ref,
    wm_ref,
    w1_ref,
    w2_ref,
    f1_ref,
    f2_ref,
    *refs,
):
    left_before, right_before = refs[:-4] if len(refs) > 4 else (None, None)
    out_ref, left_ref, right_ref, attended = refs[-4:]
    sources, count, span, channels = x_ref.shape
    rows = sources * span
    tall = count * rows
    x = jnp.concatenate(
        [x_ref[:, c].reshape(rows, channels) for c in range(count)], axis=0
    ).astype(F32)
    normed = layer_norm(x).astype(BF16)
    normed_t = normed.T
    queries_t = (dot(wq_ref[...], normed_t) * (1.0 / math.sqrt(HEAD))).astype(BF16)
    values_t = dot(wv_ref[...], normed_t).astype(BF16)
    keys = dot(normed, wk_ref[...]).astype(BF16)
    fill = fill_ref[...]
    ones = jnp.ones((16, rows), BF16)
    for h in range(HEADS):
        for c in range(count):
            cut = slice(h * HEAD, (h + 1) * HEAD)
            col = slice(c * rows, (c + 1) * rows)
            scores = dot(keys[col, cut], queries_t[cut, col]) + fill
            peak = jnp.max(scores, axis=0, keepdims=True)
            weights = jnp.exp(scores - peak)
            total = jnp.sum(weights, axis=0, keepdims=True)
            summed = dot(values_t[cut, col], weights.astype(BF16))
            attended[cut, col] = summed / total
    gate = jax.nn.sigmoid(dot(normed, wg_ref[...]))
    gated = (gate * attended[...].T).astype(BF16)
    after = (x + dot(gated, wm_ref[...])).astype(BF16)
    after_wide = after.astype(F32)
    normed = layer_norm(after_wide).astype(BF16)
    hidden = jnp.maximum(dot(normed, w1_ref[...]), 0.0).astype(BF16)
    update = (after_wide + dot(hidden, w2_ref[...])).astype(BF16)
    for c in range(count):
        out_ref[:, c] = update[c * rows : (c + 1) * rows].reshape(sources, span, channels)
    normed = layer_norm(update.astype(F32)).astype(BF16)
    left = sum(dot(normed[c * rows : (c + 1) * rows], f1_ref[c]) for c in range(count))
    right = sum(dot_nt(f2_ref[c], normed[c * rows : (c + 1) * rows]) for c in range(count))
    left = (left * row_col_ref[...] * keep_left_ref[...]).astype(BF16)
    right = (right * row_row_ref[...] * keep_right_ref[...]).astype(BF16)
    if left_before is not None:
        left += left_before[...]
        right += right_before[...]
    left_ref[...] = left
    right_ref[...] = right


def columns(x, fill, row_col, row_row, keep_left, keep_right, weights, first, count, before):
    sources, _, span, channels = x.shape
    rows = sources * span
    lanes = weights[-2].shape[2]

    def whole(a):
        return pl.BlockSpec(a.shape, lambda k, n=a.ndim: (0,) * n)

    def column(start):
        return pl.BlockSpec((sources, count, span, channels), lambda k: (0, start, 0, 0))

    smalls = (fill, row_col, row_row, keep_left, keep_right)
    specs = [column(first // count)] + [whole(a) for a in smalls] + [whole(w) for w in weights[:-2]]
    specs += [pl.BlockSpec((count,) + w.shape[1:], lambda k: (first // count, 0, 0)) for w in weights[-2:]]
    specs += [whole(b) for b in before]
    return pl.pallas_call(
        column_kernel,
        grid=(1,),
        in_specs=specs,
        out_specs=(
            column(0),
            pl.BlockSpec((rows, lanes), lambda k: (0, 0)),
            pl.BlockSpec((lanes, rows), lambda k: (0, 0)),
        ),
        out_shape=(
            jax.ShapeDtypeStruct((sources, count, span, channels), BF16),
            jax.ShapeDtypeStruct((rows, lanes), BF16),
            jax.ShapeDtypeStruct((lanes, rows), BF16),
        ),
        scratch_shapes=[
            pltpu.VMEM((channels, count * rows), F32),
        ],
        compiler_params=pltpu.CompilerParams(
            dimension_semantics=("arbitrary",), vmem_limit_bytes=28 * 2**20
        ),
        cost_estimate=pl.CostEstimate(
            flops=6 * 10**9, bytes_accessed=4 * 2**20, transcendentals=4 * 10**6
        ),
    )(x, *smalls, *weights, *before)


def pair_kernel(
    place_ref,
    pair_ref,
    scale_ref,
    left_ref,
    wo_ref,
    bias_ref,
    up_ref,
    down_ref,
    *refs,
    count,
):
    blocks = refs[: 2 * count]
    out_ref, flats, wo, tiles, made, in_sems, out_sems = refs[-7:]
    groups, rows, lanes = left_ref.shape
    width, near, _ = blocks[0].shape
    tall = width * near
    span = 2 * near
    cuts = lanes // COUPLING
    many = groups * span
    core = place_ref[count]
    spots = [pl.ds(pl.multiple_of(place_ref[n] * span, span), span) for n in range(count)]
    fetches = [pltpu.make_async_copy(wo_ref, wo, in_sems.at[count])]
    for n, spot in enumerate(spots):
        fetches.append(
            pltpu.make_async_copy(pair_ref.at[:, spot, :], tiles.at[n], in_sems.at[n])
        )
    for fetch in fetches:
        fetch.start()
    for n in range(count):
        own = blocks[2 * n][...].reshape(tall, rows)
        other = blocks[2 * n + 1][...].reshape(tall, rows)
        right = jnp.concatenate(
            [jnp.where(core == 0, own, other), jnp.where(core == 0, other, own)], axis=0
        )
        for pair in range(groups // 2):
            left = jnp.concatenate([left_ref[2 * pair], left_ref[2 * pair + 1]], axis=1)
            outer = dot(right, left)
            low, high = outer[:tall], outer[tall:]
            for half in range(2):
                cut = slice(half * lanes, (half + 1) * lanes)
                at = n * many + (2 * pair + half) * span
                for e in range(width):
                    part = slice(e * near, (e + 1) * near)
                    flats[at : at + span, e * lanes : (e + 1) * lanes] = jnp.concatenate(
                        [low[part, cut], high[part, cut]], axis=0
                    ).astype(BF16)
    for fetch in fetches:
        fetch.wait()
    projected = dot(flats[...], wo[...])
    bias = bias_ref[...]
    channels = bias.shape[1]
    stores = []
    for n, spot in enumerate(spots):
        kept = jnp.broadcast_to(scale_ref[spot, :], (span, channels))
        middle = []
        for g in range(groups):
            for k in range(cuts):
                i = g * cuts + k
                at = n * many + g * span
                block = projected[at : at + span, k * channels : (k + 1) * channels]
                scale = jnp.where(place_ref[count + 1 + i] > 0, kept, 1.0)
                middle.append(
                    (tiles[n, i].astype(F32) + (block + bias) * scale).astype(BF16)
                )
        middle = jnp.concatenate(middle, axis=0).astype(F32)
        normed = layer_norm(middle).astype(BF16)
        hidden = jnp.maximum(dot(normed, up_ref[...]), 0.0).astype(BF16)
        update = (middle + dot(hidden, down_ref[...])).astype(BF16)
        made[n] = update.reshape(groups * cuts, span, channels)
        stores.append(pltpu.make_async_copy(made.at[n], out_ref.at[:, spot, :], out_sems.at[n]))
        stores[-1].start()
    for store in stores:
        store.wait()


def pair_blocks(place, pair, scale, left, weights, blocks, before):
    count = len(blocks) // 2
    _, near, rows = blocks[0].shape
    groups, _, lanes = left.shape

    def whole(a):
        return pl.BlockSpec(a.shape, lambda i, place, n=a.ndim: (0,) * n)

    operands = [pair, scale, left, *weights, *blocks, *before]
    far = pl.BlockSpec(memory_space=pl.ANY)
    specs = [whole(a) for a in operands]
    for n in (0, 3, *range(len(operands) - len(before), len(operands))):
        specs[n] = far
    span = 2 * near
    tiles = pltpu.VMEM((count, pair.shape[0], span, pair.shape[2]), pair.dtype)
    return pl.pallas_call(
        functools.partial(pair_kernel, count=count),
        grid_spec=pltpu.PrefetchScalarGridSpec(
            num_scalar_prefetch=1,
            grid=(1,),
            in_specs=specs,
            out_specs=far,
            scratch_shapes=[
                pltpu.VMEM((count * groups * span, COUPLING * lanes), BF16),
                pltpu.VMEM(weights[0].shape, BF16),
                tiles,
                tiles,
                pltpu.SemaphoreType.DMA((count + 1,)),
                pltpu.SemaphoreType.DMA((count,)),
            ],
        ),
        out_shape=jax.ShapeDtypeStruct(pair.shape, pair.dtype),
        input_output_aliases={len(operands): 0} if before else {},
        compiler_params=pltpu.CompilerParams(
            dimension_semantics=("arbitrary",), vmem_limit_bytes=36 * 2**20
        ),
        cost_estimate=pl.CostEstimate(
            flops=count * 2 * 10**9, bytes_accessed=6 * 2**20, transcendentals=0
        ),
    )(place, *operands)


NEWPAIR = True


def ring(size, shift):
    return [(i, (i + shift) % size) for i in range(size)]


def left_route(sizes):
    zs, ys, cs, xs, ls = sizes
    pairs = []
    place = lambda z, y, c, x, l: (((z * ys + y) * cs + c) * xs + x) * ls + l
    for z in range(zs):
        for y in range(ys):
            for c in range(cs):
                for x in range(xs):
                    for l in range(ls):
                        block = z // 2
                        slot = 4 * (z % 2) + 2 * c + y
                        pairs.append(
                            (
                                place(z, y, c, x, l),
                                place(x * ls + l, block // cs, block % cs, slot // ls, slot % ls),
                            )
                        )
    return pairs


def per_device(
    homolog_embedding,
    pair_features,
    row_present_mask,
    residue_keep_mask,
    query_weight,
    key_weight,
    content_matrix,
    sigmoid_switch_matrix,
    focus_merge_matrix,
    widening_matrix,
    narrowing_matrix,
    first_factor_matrix,
    second_factor_matrix,
    outer_product_weight,
    outer_product_bias,
    pair_up_weight,
    pair_down_weight,
):
    sizes = tuple(lax.axis_size(a) for a in SEQ + RES)
    zs, ys, cs, xs, ls = sizes
    z, yh, co, xi, li = (lax.axis_index(a) for a in SEQ + RES)
    span, breadth, channels = homolog_embedding.shape
    seq_count, res_count = zs * ys * cs, xs * ls
    owned = breadth // seq_count
    rows = span * seq_count
    pair_rows, _, pair_channels = pair_features.shape
    res_index = xi * ls + li
    seq_index = (z * ys + yh) * cs + co
    flags = row_present_mask.astype(F32)
    keep = residue_keep_mask.astype(F32)

    x = homolog_embedding.reshape(span, zs, cs, ys, owned, channels)
    x = x.transpose(1, 3, 2, 4, 0, 5).reshape(seq_count, owned, span, channels)
    x = lax.all_to_all(x, SEQ, split_axis=0, concat_axis=0, tiled=True)

    row_keep = lax.dynamic_slice_in_dim(
        residue_keep_mask, seq_index * pair_rows, pair_rows, 0
    )
    col_keep = lax.dynamic_slice_in_dim(keep, res_index * breadth, breadth, 0)
    scale = (1.0 / jnp.maximum(jnp.sum(flags) * col_keep, 1.0))[:, None]
    wo = outer_product_weight.reshape(COUPLING, COUPLING, pair_channels).transpose(1, 0, 2)
    wo = jnp.where(
        (jnp.arange(owned)[:, None] == jnp.arange(owned)[None, :])[None, :, None, :, None],
        wo[:, None, :, None, :],
        jnp.zeros((), BF16),
    ).reshape(COUPLING * owned * COUPLING, owned * pair_channels)
    steps = (0, *(s * k for k in range(1, zs // 2) for s in (-1, 1)), zs // 2)
    places = jnp.stack([(z + k + zs) % zs for k in steps])
    places = [
        jnp.concatenate([part, co[None], row_keep]).astype(jnp.int32)
        for part in (places[:EARLY], places[EARLY:])
    ]
    x, wo, scale, places = lax.optimization_barrier((x, wo, scale, places))

    first = res_index * breadth + ((z * cs + co) * ys + yh) * owned
    mine = lax.dynamic_slice_in_dim(keep, first, owned, 0)
    keep_left = jnp.repeat(mine, COUPLING)[None, :]
    keep_right = jnp.tile(mine, COUPLING)[:, None]
    pad_left = jnp.zeros((owned, channels, owned, COUPLING), BF16)
    pad_right = jnp.zeros((owned, COUPLING, owned, channels), BF16)
    for k in range(owned):
        pad_left = pad_left.at[k, :, k].set(first_factor_matrix)
        pad_right = pad_right.at[k, :, k].set(second_factor_matrix.T)
    weights = (
        query_weight.T,
        key_weight,
        content_matrix.T,
        sigmoid_switch_matrix,
        focus_merge_matrix,
        widening_matrix,
        narrowing_matrix,
        pad_left.reshape(owned, channels, owned * COUPLING),
        pad_right.reshape(owned, COUPLING * owned, channels),
    )
    fill = ((flags - 1.0) * MASK_FILL)[:, None]
    updates, before = [], ()
    for n in range(PARTS):
        update, *before = columns(
            x,
            fill,
            flags[:, None],
            flags[None, :],
            keep_left,
            keep_right,
            weights,
            n * (owned // PARTS),
            owned // PARTS,
            before,
        )
        updates.append(update)
    left, right = before

    left = lax.ppermute(left, SEQ + RES, left_route(sizes))

    right = right.reshape(COUPLING, owned, rows)
    away = lax.ppermute(right, "yh", ring(ys, 1))
    right = jnp.where(
        yh == 0,
        jnp.concatenate([right, away], axis=1),
        jnp.concatenate([away, right], axis=1),
    )
    up = down = right
    blocks = [right]
    for k in range(1, zs // 2):
        if k == TIE:
            left, up, down = lax.optimization_barrier((left, up, down))
        up = lax.ppermute(up, "z", ring(zs, 1))
        down = lax.ppermute(down, "z", ring(zs, -1))
        blocks += [up, down]
    sent = lax.all_to_all(updates[0], SEQ, split_axis=0, concat_axis=0, tiled=True)
    left, sent = lax.optimization_barrier((left, sent))
    left = jnp.broadcast_to(left[None], (res_count, *left.shape))
    left = lax.all_to_all(left, RES, split_axis=0, concat_axis=0, tiled=True)
    left, up, down = lax.optimization_barrier((left, up, down))
    half = COUPLING // 2
    up = lax.ppermute(up[:half], "z", ring(zs, 1))
    down = lax.ppermute(down[half:], "z", ring(zs, -1))
    blocks = [(own, lax.ppermute(own, "co", ring(cs, 1))) for own in blocks]
    last, left = lax.optimization_barrier((updates[1], left))
    last = lax.all_to_all(last, SEQ, split_axis=0, concat_axis=0, tiled=True)
    updates = [sent, last]
    update = jnp.concatenate(updates, axis=1)
    update = update.reshape(zs, ys, cs, owned, span, channels).transpose(4, 0, 2, 1, 3, 5)
    update = update.reshape(span, breadth, channels)

    pair_weights = (wo, outer_product_bias[None, :], pair_up_weight, pair_down_weight)

    def tiles(place, few, before):
        few = [block for own, other in few for block in (own, other)]
        return pair_blocks(place, pair_features, scale, left, pair_weights, few, before)

    pair = tiles(places[0], blocks[:EARLY], ())
    up, down, pair = lax.optimization_barrier((up, down, pair))
    own = jnp.concatenate([up, down], axis=0)
    blocks.append((own, lax.ppermute(own, "co", ring(cs, 1))))
    pair = tiles(places[1], blocks[EARLY:], (pair,))
    return update, pair


def solution(mesh):
    grid = mesh.devices.reshape(8, 2, 2, 4, 2)
    fine = Mesh(grid, SEQ + RES)
    split = P(SEQ, RES, None)
    return jax.shard_map(
        per_device,
        mesh=fine,
        in_specs=(split, split) + (P(),) * 15,
        out_specs=(split, split),
        check_vma=False,
    )
```

```python
import functools
import math

import jax
import jax.numpy as jnp
from jax import lax
from jax.experimental import pallas as pl
from jax.experimental.pallas import tpu as pltpu
from jax.sharding import Mesh, PartitionSpec as P

HEADS = 8
HEAD = 32
COUPLING = 32
PARTS = 2
EARLY = 5
TIE = 1
EPSILON = 1e-05
MASK_FILL = 1000000000.0
SEQ = ("z", "yh", "co")
RES = ("x", "yl")
F32 = jnp.float32
BF16 = jnp.bfloat16


def layer_norm(values):
    centre = values - jnp.mean(values, axis=-1, keepdims=True)
    spread = jnp.mean(centre * centre, axis=-1, keepdims=True)
    return centre * lax.rsqrt(spread + EPSILON)


def dot(a, b):
    return jnp.dot(a, b, preferred_element_type=F32)


def dot_nt(a, b):
    return lax.dot_general(a, b, (((1,), (1,)), ((), ())), preferred_element_type=F32)


def column_kernel(
    x_ref,
    fill_ref,
    row_col_ref,
    row_row_ref,
    keep_left_ref,
    keep_right_ref,
    wq_ref,
    wk_ref,
    wv_ref,
    wg_ref,
    wm_ref,
    w1_ref,
    w2_ref,
    f1_ref,
    f2_ref,
    out_ref,
    left_ref,
    right_ref,
    attended,
):
    step = pl.program_id(0)
    sources, count, span, channels = x_ref.shape
    rows = sources * span
    tall = count * rows
    x = jnp.concatenate(
        [x_ref[:, c].reshape(rows, channels) for c in range(count)], axis=0
    ).astype(F32)
    normed = layer_norm(x).astype(BF16)
    normed_t = normed.T
    queries_t = (dot(wq_ref[...], normed_t) * (1.0 / math.sqrt(HEAD))).astype(BF16)
    values_t = dot(wv_ref[...], normed_t).astype(BF16)
    keys = dot(normed, wk_ref[...]).astype(BF16)
    fill = fill_ref[...]
    ones = jnp.ones((16, rows), BF16)
    for h in range(HEADS):
        for c in range(count):
            cut = slice(h * HEAD, (h + 1) * HEAD)
            col = slice(c * rows, (c + 1) * rows)
            scores = dot(keys[col, cut], queries_t[cut, col]) + fill
            peak = jnp.max(scores, axis=0, keepdims=True)
            weights = jnp.exp(scores - peak)
            total = jnp.sum(weights, axis=0, keepdims=True)
            summed = dot(values_t[cut, col], weights.astype(BF16))
            attended[cut, col] = summed / total
    gate = jax.nn.sigmoid(dot(normed, wg_ref[...]))
    gated = (gate * attended[...].T).astype(BF16)
    after = (x + dot(gated, wm_ref[...])).astype(BF16)
    after_wide = after.astype(F32)
    normed = layer_norm(after_wide).astype(BF16)
    hidden = jnp.maximum(dot(normed, w1_ref[...]), 0.0).astype(BF16)
    update = (after_wide + dot(hidden, w2_ref[...])).astype(BF16)
    for c in range(count):
        out_ref[:, c] = update[c * rows : (c + 1) * rows].reshape(sources, span, channels)
    normed = layer_norm(update.astype(F32)).astype(BF16)
    left = sum(dot(normed[c * rows : (c + 1) * rows], f1_ref[c]) for c in range(count))
    right = sum(dot_nt(f2_ref[c], normed[c * rows : (c + 1) * rows]) for c in range(count))
    left = (left * row_col_ref[...] * keep_left_ref[...]).astype(BF16)
    right = (right * row_row_ref[...] * keep_right_ref[...]).astype(BF16)

    @pl.when(step == 0)
    def _():
        left_ref[...] = left
        right_ref[...] = right

    @pl.when(step > 0)
    def _():
        left_ref[...] += left
        right_ref[...] += right


def columns(x, fill, row_col, row_row, keep_left, keep_right, weights, count):
    sources, owned, span, channels = x.shape
    rows = sources * span
    lanes = weights[-2].shape[2]

    def whole(a):
        return pl.BlockSpec(a.shape, lambda k, n=a.ndim: (0,) * n)

    column = pl.BlockSpec((sources, count, span, channels), lambda k: (0, k, 0, 0))
    smalls = (fill, row_col, row_row, keep_left, keep_right)
    specs = [column] + [whole(a) for a in smalls] + [whole(w) for w in weights[:-2]]
    specs += [pl.BlockSpec((count,) + w.shape[1:], lambda k: (k, 0, 0)) for w in weights[-2:]]
    return pl.pallas_call(
        column_kernel,
        grid=(owned // count,),
        in_specs=specs,
        out_specs=(
            column,
            pl.BlockSpec((rows, lanes), lambda k: (0, 0)),
            pl.BlockSpec((lanes, rows), lambda k: (0, 0)),
        ),
        out_shape=(
            jax.ShapeDtypeStruct(x.shape, BF16),
            jax.ShapeDtypeStruct((rows, lanes), BF16),
            jax.ShapeDtypeStruct((lanes, rows), BF16),
        ),
        scratch_shapes=[
            pltpu.VMEM((channels, count * rows), F32),
        ],
        compiler_params=pltpu.CompilerParams(
            dimension_semantics=("arbitrary",), vmem_limit_bytes=32 * 2**20
        ),
        cost_estimate=pl.CostEstimate(
            flops=6 * 10**9, bytes_accessed=4 * 2**20, transcendentals=4 * 10**6
        ),
    )(x, *smalls, *weights)


def pair_kernel(
    place_ref,
    pair_ref,
    scale_ref,
    left_ref,
    wo_ref,
    bias_ref,
    up_ref,
    down_ref,
    *refs,
    count,
):
    blocks = refs[: 2 * count]
    out_ref, flats, wo, tiles, made, in_sems, out_sems = refs[-7:]
    groups, rows, lanes = left_ref.shape
    width, near, _ = blocks[0].shape
    tall = width * near
    span = 2 * near
    cuts = lanes // COUPLING
    many = groups * span
    core = place_ref[count]
    spots = [pl.ds(pl.multiple_of(place_ref[n] * span, span), span) for n in range(count)]
    fetches = [pltpu.make_async_copy(wo_ref, wo, in_sems.at[count])]
    for n, spot in enumerate(spots):
        fetches.append(
            pltpu.make_async_copy(pair_ref.at[:, spot, :], tiles.at[n], in_sems.at[n])
        )
    for fetch in fetches:
        fetch.start()
    for n in range(count):
        own = blocks[2 * n][...].reshape(tall, rows)
        other = blocks[2 * n + 1][...].reshape(tall, rows)
        right = jnp.concatenate(
            [jnp.where(core == 0, own, other), jnp.where(core == 0, other, own)], axis=0
        )
        for pair in range(groups // 2):
            left = jnp.concatenate([left_ref[2 * pair], left_ref[2 * pair + 1]], axis=1)
            outer = dot(right, left)
            low, high = outer[:tall], outer[tall:]
            for half in range(2):
                cut = slice(half * lanes, (half + 1) * lanes)
                at = n * many + (2 * pair + half) * span
                for e in range(width):
                    part = slice(e * near, (e + 1) * near)
                    flats[at : at + span, e * lanes : (e + 1) * lanes] = jnp.concatenate(
                        [low[part, cut], high[part, cut]], axis=0
                    ).astype(BF16)
    for fetch in fetches:
        fetch.wait()
    projected = dot(flats[...], wo[...])
    bias = bias_ref[...]
    channels = bias.shape[1]
    stores = []
    for n, spot in enumerate(spots):
        kept = jnp.broadcast_to(scale_ref[spot, :], (span, channels))
        middle = []
        for g in range(groups):
            for k in range(cuts):
                i = g * cuts + k
                at = n * many + g * span
                block = projected[at : at + span, k * channels : (k + 1) * channels]
                scale = jnp.where(place_ref[count + 1 + i] > 0, kept, 1.0)
                middle.append(
                    (tiles[n, i].astype(F32) + (block + bias) * scale).astype(BF16)
                )
        middle = jnp.concatenate(middle, axis=0).astype(F32)
        normed = layer_norm(middle).astype(BF16)
        hidden = jnp.maximum(dot(normed, up_ref[...]), 0.0).astype(BF16)
        update = (middle + dot(hidden, down_ref[...])).astype(BF16)
        made[n] = update.reshape(groups * cuts, span, channels)
        stores.append(pltpu.make_async_copy(made.at[n], out_ref.at[:, spot, :], out_sems.at[n]))
        stores[-1].start()
    for store in stores:
        store.wait()


def pair_blocks(place, pair, scale, left, weights, blocks, before):
    count = len(blocks) // 2
    _, near, rows = blocks[0].shape
    groups, _, lanes = left.shape

    def whole(a):
        return pl.BlockSpec(a.shape, lambda i, place, n=a.ndim: (0,) * n)

    operands = [pair, scale, left, *weights, *blocks, *before]
    far = pl.BlockSpec(memory_space=pl.ANY)
    specs = [whole(a) for a in operands]
    for n in (0, 3, *range(len(operands) - len(before), len(operands))):
        specs[n] = far
    span = 2 * near
    tiles = pltpu.VMEM((count, pair.shape[0], span, pair.shape[2]), pair.dtype)
    return pl.pallas_call(
        functools.partial(pair_kernel, count=count),
        grid_spec=pltpu.PrefetchScalarGridSpec(
            num_scalar_prefetch=1,
            grid=(1,),
            in_specs=specs,
            out_specs=far,
            scratch_shapes=[
                pltpu.VMEM((count * groups * span, COUPLING * lanes), BF16),
                pltpu.VMEM(weights[0].shape, BF16),
                tiles,
                tiles,
                pltpu.SemaphoreType.DMA((count + 1,)),
                pltpu.SemaphoreType.DMA((count,)),
            ],
        ),
        out_shape=jax.ShapeDtypeStruct(pair.shape, pair.dtype),
        input_output_aliases={len(operands): 0} if before else {},
        compiler_params=pltpu.CompilerParams(
            dimension_semantics=("arbitrary",), vmem_limit_bytes=36 * 2**20
        ),
        cost_estimate=pl.CostEstimate(
            flops=count * 2 * 10**9, bytes_accessed=6 * 2**20, transcendentals=0
        ),
    )(place, *operands)


NEWPAIR = True


def ring(size, shift):
    return [(i, (i + shift) % size) for i in range(size)]


def left_route(sizes):
    zs, ys, cs, xs, ls = sizes
    pairs = []
    place = lambda z, y, c, x, l: (((z * ys + y) * cs + c) * xs + x) * ls + l
    for z in range(zs):
        for y in range(ys):
            for c in range(cs):
                for x in range(xs):
                    for l in range(ls):
                        block = z // 2
                        slot = 4 * (z % 2) + 2 * c + y
                        pairs.append(
                            (
                                place(z, y, c, x, l),
                                place(x * ls + l, block // cs, block % cs, slot // ls, slot % ls),
                            )
                        )
    return pairs


def per_device(
    homolog_embedding,
    pair_features,
    row_present_mask,
    residue_keep_mask,
    query_weight,
    key_weight,
    content_matrix,
    sigmoid_switch_matrix,
    focus_merge_matrix,
    widening_matrix,
    narrowing_matrix,
    first_factor_matrix,
    second_factor_matrix,
    outer_product_weight,
    outer_product_bias,
    pair_up_weight,
    pair_down_weight,
):
    sizes = tuple(lax.axis_size(a) for a in SEQ + RES)
    zs, ys, cs, xs, ls = sizes
    z, yh, co, xi, li = (lax.axis_index(a) for a in SEQ + RES)
    span, breadth, channels = homolog_embedding.shape
    seq_count, res_count = zs * ys * cs, xs * ls
    owned = breadth // seq_count
    rows = span * seq_count
    pair_rows, _, pair_channels = pair_features.shape
    res_index = xi * ls + li
    seq_index = (z * ys + yh) * cs + co
    flags = row_present_mask.astype(F32)
    keep = residue_keep_mask.astype(F32)

    x = homolog_embedding.reshape(span, zs, cs, ys, owned, channels)
    x = x.transpose(1, 3, 2, 4, 0, 5).reshape(seq_count, owned, span, channels)
    x = lax.all_to_all(x, SEQ, split_axis=0, concat_axis=0, tiled=True)

    row_keep = lax.dynamic_slice_in_dim(
        residue_keep_mask, seq_index * pair_rows, pair_rows, 0
    )
    col_keep = lax.dynamic_slice_in_dim(keep, res_index * breadth, breadth, 0)
    scale = (1.0 / jnp.maximum(jnp.sum(flags) * col_keep, 1.0))[:, None]
    wo = outer_product_weight.reshape(COUPLING, COUPLING, pair_channels).transpose(1, 0, 2)
    wo = jnp.where(
        (jnp.arange(owned)[:, None] == jnp.arange(owned)[None, :])[None, :, None, :, None],
        wo[:, None, :, None, :],
        jnp.zeros((), BF16),
    ).reshape(COUPLING * owned * COUPLING, owned * pair_channels)
    steps = (0, *(s * k for k in range(1, zs // 2) for s in (-1, 1)), zs // 2)
    places = jnp.stack([(z + k + zs) % zs for k in steps])
    places = [
        jnp.concatenate([part, co[None], row_keep]).astype(jnp.int32)
        for part in (places[:EARLY], places[EARLY:])
    ]
    x, wo, scale, places = lax.optimization_barrier((x, wo, scale, places))

    first = res_index * breadth + ((z * cs + co) * ys + yh) * owned
    mine = lax.dynamic_slice_in_dim(keep, first, owned, 0)
    keep_left = jnp.repeat(mine, COUPLING)[None, :]
    keep_right = jnp.tile(mine, COUPLING)[:, None]
    pad_left = jnp.zeros((owned, channels, owned, COUPLING), BF16)
    pad_right = jnp.zeros((owned, COUPLING, owned, channels), BF16)
    for k in range(owned):
        pad_left = pad_left.at[k, :, k].set(first_factor_matrix)
        pad_right = pad_right.at[k, :, k].set(second_factor_matrix.T)
    weights = (
        query_weight.T,
        key_weight,
        content_matrix.T,
        sigmoid_switch_matrix,
        focus_merge_matrix,
        widening_matrix,
        narrowing_matrix,
        pad_left.reshape(owned, channels, owned * COUPLING),
        pad_right.reshape(owned, COUPLING * owned, channels),
    )
    fill = ((flags - 1.0) * MASK_FILL)[:, None]
    update, left, right = columns(
        x,
        fill,
        flags[:, None],
        flags[None, :],
        keep_left,
        keep_right,
        weights,
        owned // PARTS,
    )
    update = lax.all_to_all(update, SEQ, split_axis=0, concat_axis=0, tiled=True)

    left = lax.ppermute(left, SEQ + RES, left_route(sizes))

    right = right.reshape(COUPLING, owned, rows)
    away = lax.ppermute(right, "yh", ring(ys, 1))
    right = jnp.where(
        yh == 0,
        jnp.concatenate([right, away], axis=1),
        jnp.concatenate([away, right], axis=1),
    )
    up = down = right
    blocks = [right]
    for k in range(1, zs // 2):
        if k == TIE:
            left, up, down = lax.optimization_barrier((left, up, down))
        up = lax.ppermute(up, "z", ring(zs, 1))
        down = lax.ppermute(down, "z", ring(zs, -1))
        blocks += [up, down]
    left, update = lax.optimization_barrier((left, update))
    left = jnp.broadcast_to(left[None], (res_count, *left.shape))
    left = lax.all_to_all(left, RES, split_axis=0, concat_axis=0, tiled=True)
    update = update.reshape(zs, ys, cs, owned, span, channels).transpose(4, 0, 2, 1, 3, 5)
    update = update.reshape(span, breadth, channels)
    left, up, down, update = lax.optimization_barrier((left, up, down, update))
    half = COUPLING // 2
    up = lax.ppermute(up[:half], "z", ring(zs, 1))
    down = lax.ppermute(down[half:], "z", ring(zs, -1))
    blocks = [(own, lax.ppermute(own, "co", ring(cs, 1))) for own in blocks]

    pair_weights = (wo, outer_product_bias[None, :], pair_up_weight, pair_down_weight)

    def tiles(place, few, before):
        few = [block for own, other in few for block in (own, other)]
        return pair_blocks(place, pair_features, scale, left, pair_weights, few, before)

    pair = tiles(places[0], blocks[:EARLY], ())
    up, down, pair = lax.optimization_barrier((up, down, pair))
    own = jnp.concatenate([up, down], axis=0)
    blocks.append((own, lax.ppermute(own, "co", ring(cs, 1))))
    pair = tiles(places[1], blocks[EARLY:], (pair,))
    return update, pair


def solution(mesh):
    grid = mesh.devices.reshape(8, 2, 2, 4, 2)
    fine = Mesh(grid, SEQ + RES)
    split = P(SEQ, RES, None)
    return jax.shard_map(
        per_device,
        mesh=fine,
        in_specs=(split, split) + (P(),) * 15,
        out_specs=(split, split),
        check_vma=False,
    )
```

```python
import functools
import math

import jax
import jax.numpy as jnp
from jax import lax
from jax.experimental import pallas as pl
from jax.experimental.pallas import tpu as pltpu
from jax.sharding import Mesh, PartitionSpec as P

HEADS = 8
HEAD = 32
COUPLING = 32
PARTS = 2
EARLY = 5
TIE = 2
EPSILON = 1e-05
MASK_FILL = 1000000000.0
SEQ = ("z", "yh", "co")
RES = ("x", "yl")
F32 = jnp.float32
BF16 = jnp.bfloat16


def layer_norm(values):
    centre = values - jnp.mean(values, axis=-1, keepdims=True)
    spread = jnp.mean(centre * centre, axis=-1, keepdims=True)
    return centre * lax.rsqrt(spread + EPSILON)


def dot(a, b):
    return jnp.dot(a, b, preferred_element_type=F32)


def dot_nt(a, b):
    return lax.dot_general(a, b, (((1,), (1,)), ((), ())), preferred_element_type=F32)


def column_kernel(
    x_ref,
    fill_ref,
    row_col_ref,
    row_row_ref,
    keep_left_ref,
    keep_right_ref,
    wq_ref,
    wk_ref,
    wv_ref,
    wg_ref,
    wm_ref,
    w1_ref,
    w2_ref,
    f1_ref,
    f2_ref,
    out_ref,
    left_ref,
    right_ref,
    attended,
):
    step = pl.program_id(0)
    sources, count, span, channels = x_ref.shape
    rows = sources * span
    tall = count * rows
    x = jnp.concatenate(
        [x_ref[:, c].reshape(rows, channels) for c in range(count)], axis=0
    ).astype(F32)
    normed = layer_norm(x).astype(BF16)
    normed_t = normed.T
    queries_t = (dot(wq_ref[...], normed_t) * (1.0 / math.sqrt(HEAD))).astype(BF16)
    values_t = dot(wv_ref[...], normed_t).astype(BF16)
    keys = dot(normed, wk_ref[...]).astype(BF16)
    fill = fill_ref[...]
    ones = jnp.ones((16, rows), BF16)
    for h in range(HEADS):
        for c in range(count):
            cut = slice(h * HEAD, (h + 1) * HEAD)
            col = slice(c * rows, (c + 1) * rows)
            scores = dot(keys[col, cut], queries_t[cut, col]) + fill
            peak = jnp.max(scores, axis=0, keepdims=True)
            weights = jnp.exp(scores - peak)
            total = jnp.sum(weights, axis=0, keepdims=True)
            summed = dot(values_t[cut, col], weights.astype(BF16))
            attended[cut, col] = summed / total
    gate = jax.nn.sigmoid(dot(normed, wg_ref[...]))
    gated = (gate * attended[...].T).astype(BF16)
    after = (x + dot(gated, wm_ref[...])).astype(BF16)
    after_wide = after.astype(F32)
    normed = layer_norm(after_wide).astype(BF16)
    hidden = jnp.maximum(dot(normed, w1_ref[...]), 0.0).astype(BF16)
    update = (after_wide + dot(hidden, w2_ref[...])).astype(BF16)
    for c in range(count):
        out_ref[:, c] = update[c * rows : (c + 1) * rows].reshape(sources, span, channels)
    normed = layer_norm(update.astype(F32)).astype(BF16)
    left = sum(dot(normed[c * rows : (c + 1) * rows], f1_ref[c]) for c in range(count))
    right = sum(dot_nt(f2_ref[c], normed[c * rows : (c + 1) * rows]) for c in range(count))
    left = (left * row_col_ref[...] * keep_left_ref[...]).astype(BF16)
    right = (right * row_row_ref[...] * keep_right_ref[...]).astype(BF16)

    @pl.when(step == 0)
    def _():
        left_ref[...] = left
        right_ref[...] = right

    @pl.when(step > 0)
    def _():
        left_ref[...] += left
        right_ref[...] += right


def columns(x, fill, row_col, row_row, keep_left, keep_right, weights, count):
    sources, owned, span, channels = x.shape
    rows = sources * span
    lanes = weights[-2].shape[2]

    def whole(a):
        return pl.BlockSpec(a.shape, lambda k, n=a.ndim: (0,) * n)

    column = pl.BlockSpec((sources, count, span, channels), lambda k: (0, k, 0, 0))
    smalls = (fill, row_col, row_row, keep_left, keep_right)
    specs = [column] + [whole(a) for a in smalls] + [whole(w) for w in weights[:-2]]
    specs += [pl.BlockSpec((count,) + w.shape[1:], lambda k: (k, 0, 0)) for w in weights[-2:]]
    return pl.pallas_call(
        column_kernel,
        grid=(owned // count,),
        in_specs=specs,
        out_specs=(
            column,
            pl.BlockSpec((rows, lanes), lambda k: (0, 0)),
            pl.BlockSpec((lanes, rows), lambda k: (0, 0)),
        ),
        out_shape=(
            jax.ShapeDtypeStruct(x.shape, BF16),
            jax.ShapeDtypeStruct((rows, lanes), BF16),
            jax.ShapeDtypeStruct((lanes, rows), BF16),
        ),
        scratch_shapes=[
            pltpu.VMEM((channels, count * rows), F32),
        ],
        compiler_params=pltpu.CompilerParams(
            dimension_semantics=("arbitrary",), vmem_limit_bytes=32 * 2**20
        ),
        cost_estimate=pl.CostEstimate(
            flops=6 * 10**9, bytes_accessed=4 * 2**20, transcendentals=4 * 10**6
        ),
    )(x, *smalls, *weights)


def pair_kernel(
    place_ref,
    pair_ref,
    scale_ref,
    left_ref,
    wo_ref,
    bias_ref,
    up_ref,
    down_ref,
    *refs,
    count,
):
    blocks = refs[: 2 * count]
    out_ref, flats, wo, tiles, made, in_sems, out_sems = refs[-7:]
    groups, rows, lanes = left_ref.shape
    width, near, _ = blocks[0].shape
    tall = width * near
    span = 2 * near
    cuts = lanes // COUPLING
    many = groups * span
    core = place_ref[count]
    spots = [pl.ds(pl.multiple_of(place_ref[n] * span, span), span) for n in range(count)]
    fetches = [pltpu.make_async_copy(wo_ref, wo, in_sems.at[count])]
    for n, spot in enumerate(spots):
        fetches.append(
            pltpu.make_async_copy(pair_ref.at[:, spot, :], tiles.at[n], in_sems.at[n])
        )
    for fetch in fetches:
        fetch.start()
    for n in range(count):
        own = blocks[2 * n][...].reshape(tall, rows)
        other = blocks[2 * n + 1][...].reshape(tall, rows)
        right = jnp.concatenate(
            [jnp.where(core == 0, own, other), jnp.where(core == 0, other, own)], axis=0
        )
        for pair in range(groups // 2):
            left = jnp.concatenate([left_ref[2 * pair], left_ref[2 * pair + 1]], axis=1)
            outer = dot(right, left)
            low, high = outer[:tall], outer[tall:]
            for half in range(2):
                cut = slice(half * lanes, (half + 1) * lanes)
                at = n * many + (2 * pair + half) * span
                for e in range(width):
                    part = slice(e * near, (e + 1) * near)
                    flats[at : at + span, e * lanes : (e + 1) * lanes] = jnp.concatenate(
                        [low[part, cut], high[part, cut]], axis=0
                    ).astype(BF16)
    for fetch in fetches:
        fetch.wait()
    projected = dot(flats[...], wo[...])
    bias = bias_ref[...]
    channels = bias.shape[1]
    stores = []
    for n, spot in enumerate(spots):
        kept = jnp.broadcast_to(scale_ref[spot, :], (span, channels))
        middle = []
        for g in range(groups):
            for k in range(cuts):
                i = g * cuts + k
                at = n * many + g * span
                block = projected[at : at + span, k * channels : (k + 1) * channels]
                scale = jnp.where(place_ref[count + 1 + i] > 0, kept, 1.0)
                middle.append(
                    (tiles[n, i].astype(F32) + (block + bias) * scale).astype(BF16)
                )
        middle = jnp.concatenate(middle, axis=0).astype(F32)
        normed = layer_norm(middle).astype(BF16)
        hidden = jnp.maximum(dot(normed, up_ref[...]), 0.0).astype(BF16)
        update = (middle + dot(hidden, down_ref[...])).astype(BF16)
        made[n] = update.reshape(groups * cuts, span, channels)
        stores.append(pltpu.make_async_copy(made.at[n], out_ref.at[:, spot, :], out_sems.at[n]))
        stores[-1].start()
    for store in stores:
        store.wait()


def pair_blocks(place, pair, scale, left, weights, blocks, before):
    count = len(blocks) // 2
    _, near, rows = blocks[0].shape
    groups, _, lanes = left.shape

    def whole(a):
        return pl.BlockSpec(a.shape, lambda i, place, n=a.ndim: (0,) * n)

    operands = [pair, scale, left, *weights, *blocks, *before]
    far = pl.BlockSpec(memory_space=pl.ANY)
    specs = [whole(a) for a in operands]
    for n in (0, 3, *range(len(operands) - len(before), len(operands))):
        specs[n] = far
    span = 2 * near
    tiles = pltpu.VMEM((count, pair.shape[0], span, pair.shape[2]), pair.dtype)
    return pl.pallas_call(
        functools.partial(pair_kernel, count=count),
        grid_spec=pltpu.PrefetchScalarGridSpec(
            num_scalar_prefetch=1,
            grid=(1,),
            in_specs=specs,
            out_specs=far,
            scratch_shapes=[
                pltpu.VMEM((count * groups * span, COUPLING * lanes), BF16),
                pltpu.VMEM(weights[0].shape, BF16),
                tiles,
                tiles,
                pltpu.SemaphoreType.DMA((count + 1,)),
                pltpu.SemaphoreType.DMA((count,)),
            ],
        ),
        out_shape=jax.ShapeDtypeStruct(pair.shape, pair.dtype),
        input_output_aliases={len(operands): 0} if before else {},
        compiler_params=pltpu.CompilerParams(
            dimension_semantics=("arbitrary",), vmem_limit_bytes=36 * 2**20
        ),
        cost_estimate=pl.CostEstimate(
            flops=count * 2 * 10**9, bytes_accessed=6 * 2**20, transcendentals=0
        ),
    )(place, *operands)


NEWPAIR = True


def ring(size, shift):
    return [(i, (i + shift) % size) for i in range(size)]


def left_route(sizes):
    zs, ys, cs, xs, ls = sizes
    pairs = []
    place = lambda z, y, c, x, l: (((z * ys + y) * cs + c) * xs + x) * ls + l
    for z in range(zs):
        for y in range(ys):
            for c in range(cs):
                for x in range(xs):
                    for l in range(ls):
                        block = z // 2
                        slot = 4 * (z % 2) + 2 * c + y
                        pairs.append(
                            (
                                place(z, y, c, x, l),
                                place(x * ls + l, block // cs, block % cs, slot // ls, slot % ls),
                            )
                        )
    return pairs


def per_device(
    homolog_embedding,
    pair_features,
    row_present_mask,
    residue_keep_mask,
    query_weight,
    key_weight,
    content_matrix,
    sigmoid_switch_matrix,
    focus_merge_matrix,
    widening_matrix,
    narrowing_matrix,
    first_factor_matrix,
    second_factor_matrix,
    outer_product_weight,
    outer_product_bias,
    pair_up_weight,
    pair_down_weight,
):
    sizes = tuple(lax.axis_size(a) for a in SEQ + RES)
    zs, ys, cs, xs, ls = sizes
    z, yh, co, xi, li = (lax.axis_index(a) for a in SEQ + RES)
    span, breadth, channels = homolog_embedding.shape
    seq_count, res_count = zs * ys * cs, xs * ls
    owned = breadth // seq_count
    rows = span * seq_count
    pair_rows, _, pair_channels = pair_features.shape
    res_index = xi * ls + li
    seq_index = (z * ys + yh) * cs + co
    flags = row_present_mask.astype(F32)
    keep = residue_keep_mask.astype(F32)

    x = homolog_embedding.reshape(span, zs, cs, ys, owned, channels)
    x = x.transpose(1, 3, 2, 4, 0, 5).reshape(seq_count, owned, span, channels)
    x = lax.all_to_all(x, SEQ, split_axis=0, concat_axis=0, tiled=True)

    row_keep = lax.dynamic_slice_in_dim(
        residue_keep_mask, seq_index * pair_rows, pair_rows, 0
    )
    col_keep = lax.dynamic_slice_in_dim(keep, res_index * breadth, breadth, 0)
    scale = (1.0 / jnp.maximum(jnp.sum(flags) * col_keep, 1.0))[:, None]
    wo = outer_product_weight.reshape(COUPLING, COUPLING, pair_channels).transpose(1, 0, 2)
    wo = jnp.where(
        (jnp.arange(owned)[:, None] == jnp.arange(owned)[None, :])[None, :, None, :, None],
        wo[:, None, :, None, :],
        jnp.zeros((), BF16),
    ).reshape(COUPLING * owned * COUPLING, owned * pair_channels)
    steps = (0, *(s * k for k in range(1, zs // 2) for s in (-1, 1)), zs // 2)
    places = jnp.stack([(z + k + zs) % zs for k in steps])
    places = [
        jnp.concatenate([part, co[None], row_keep]).astype(jnp.int32)
        for part in (places[:EARLY], places[EARLY:])
    ]
    x, wo, scale, places = lax.optimization_barrier((x, wo, scale, places))

    first = res_index * breadth + ((z * cs + co) * ys + yh) * owned
    mine = lax.dynamic_slice_in_dim(keep, first, owned, 0)
    keep_left = jnp.repeat(mine, COUPLING)[None, :]
    keep_right = jnp.tile(mine, COUPLING)[:, None]
    pad_left = jnp.zeros((owned, channels, owned, COUPLING), BF16)
    pad_right = jnp.zeros((owned, COUPLING, owned, channels), BF16)
    for k in range(owned):
        pad_left = pad_left.at[k, :, k].set(first_factor_matrix)
        pad_right = pad_right.at[k, :, k].set(second_factor_matrix.T)
    weights = (
        query_weight.T,
        key_weight,
        content_matrix.T,
        sigmoid_switch_matrix,
        focus_merge_matrix,
        widening_matrix,
        narrowing_matrix,
        pad_left.reshape(owned, channels, owned * COUPLING),
        pad_right.reshape(owned, COUPLING * owned, channels),
    )
    fill = ((flags - 1.0) * MASK_FILL)[:, None]
    update, left, right = columns(
        x,
        fill,
        flags[:, None],
        flags[None, :],
        keep_left,
        keep_right,
        weights,
        owned // PARTS,
    )
    update = lax.all_to_all(update, SEQ, split_axis=0, concat_axis=0, tiled=True)

    left = lax.ppermute(left, SEQ + RES, left_route(sizes))

    right = right.reshape(COUPLING, owned, rows)
    away = lax.ppermute(right, "yh", ring(ys, 1))
    right = jnp.where(
        yh == 0,
        jnp.concatenate([right, away], axis=1),
        jnp.concatenate([away, right], axis=1),
    )
    up = down = right
    blocks = [right]
    for k in range(1, zs // 2):
        if k == TIE:
            left, up, down = lax.optimization_barrier((left, up, down))
        up = lax.ppermute(up, "z", ring(zs, 1))
        down = lax.ppermute(down, "z", ring(zs, -1))
        blocks += [up, down]
    left, update = lax.optimization_barrier((left, update))
    left = jnp.broadcast_to(left[None], (res_count, *left.shape))
    left = lax.all_to_all(left, RES, split_axis=0, concat_axis=0, tiled=True)
    update = update.reshape(zs, ys, cs, owned, span, channels).transpose(4, 0, 2, 1, 3, 5)
    update = update.reshape(span, breadth, channels)
    half = COUPLING // 2
    up = lax.ppermute(up[:half], "z", ring(zs, 1))
    down = lax.ppermute(down[half:], "z", ring(zs, -1))
    blocks = [(own, lax.ppermute(own, "co", ring(cs, 1))) for own in blocks]

    pair_weights = (wo, outer_product_bias[None, :], pair_up_weight, pair_down_weight)

    def tiles(place, few, before):
        few = [block for own, other in few for block in (own, other)]
        return pair_blocks(place, pair_features, scale, left, pair_weights, few, before)

    pair = tiles(places[0], blocks[:EARLY], ())
    up, down, pair = lax.optimization_barrier((up, down, pair))
    own = jnp.concatenate([up, down], axis=0)
    blocks.append((own, lax.ppermute(own, "co", ring(cs, 1))))
    pair = tiles(places[1], blocks[EARLY:], (pair,))
    return update, pair


def solution(mesh):
    grid = mesh.devices.reshape(8, 2, 2, 4, 2)
    fine = Mesh(grid, SEQ + RES)
    split = P(SEQ, RES, None)
    return jax.shard_map(
        per_device,
        mesh=fine,
        in_specs=(split, split) + (P(),) * 15,
        out_specs=(split, split),
        check_vma=False,
    )
```

```python
import functools
import math

import jax
import jax.numpy as jnp
from jax import lax
from jax.experimental import pallas as pl
from jax.experimental.pallas import tpu as pltpu
from jax.sharding import Mesh, PartitionSpec as P

HEADS = 8
HEAD = 32
COUPLING = 32
PARTS = 2
EARLY = 5
TIE = 1
EPSILON = 1e-05
MASK_FILL = 1000000000.0
SEQ = ("z", "yh", "co")
RES = ("x", "yl")
F32 = jnp.float32
BF16 = jnp.bfloat16


def layer_norm(values):
    centre = values - jnp.mean(values, axis=-1, keepdims=True)
    spread = jnp.mean(centre * centre, axis=-1, keepdims=True)
    return centre * lax.rsqrt(spread + EPSILON)


def dot(a, b):
    return jnp.dot(a, b, preferred_element_type=F32)


def dot_nt(a, b):
    return lax.dot_general(a, b, (((1,), (1,)), ((), ())), preferred_element_type=F32)


def column_kernel(
    x_ref,
    fill_ref,
    row_col_ref,
    row_row_ref,
    keep_left_ref,
    keep_right_ref,
    wq_ref,
    wk_ref,
    wv_ref,
    wg_ref,
    wm_ref,
    w1_ref,
    w2_ref,
    f1_ref,
    f2_ref,
    out_ref,
    left_ref,
    right_ref,
    attended,
):
    step = pl.program_id(0)
    sources, count, span, channels = x_ref.shape
    rows = sources * span
    tall = count * rows
    x = jnp.concatenate(
        [x_ref[:, c].reshape(rows, channels) for c in range(count)], axis=0
    ).astype(F32)
    normed = layer_norm(x).astype(BF16)
    normed_t = normed.T
    queries_t = (dot(wq_ref[...], normed_t) * (1.0 / math.sqrt(HEAD))).astype(BF16)
    values_t = dot(wv_ref[...], normed_t).astype(BF16)
    keys = dot(normed, wk_ref[...]).astype(BF16)
    fill = fill_ref[...]
    ones = jnp.ones((16, rows), BF16)
    for h in range(HEADS):
        for c in range(count):
            cut = slice(h * HEAD, (h + 1) * HEAD)
            col = slice(c * rows, (c + 1) * rows)
            scores = dot(keys[col, cut], queries_t[cut, col]) + fill
            peak = jnp.max(scores, axis=0, keepdims=True)
            weights = jnp.exp(scores - peak)
            total = jnp.sum(weights, axis=0, keepdims=True)
            summed = dot(values_t[cut, col], weights.astype(BF16))
            attended[cut, col] = summed / total
    gate = jax.nn.sigmoid(dot(normed, wg_ref[...]))
    gated = (gate * attended[...].T).astype(BF16)
    after = (x + dot(gated, wm_ref[...])).astype(BF16)
    after_wide = after.astype(F32)
    normed = layer_norm(after_wide).astype(BF16)
    hidden = jnp.maximum(dot(normed, w1_ref[...]), 0.0).astype(BF16)
    update = (after_wide + dot(hidden, w2_ref[...])).astype(BF16)
    for c in range(count):
        out_ref[:, c] = update[c * rows : (c + 1) * rows].reshape(sources, span, channels)
    normed = layer_norm(update.astype(F32)).astype(BF16)
    left = sum(dot(normed[c * rows : (c + 1) * rows], f1_ref[c]) for c in range(count))
    right = sum(dot_nt(f2_ref[c], normed[c * rows : (c + 1) * rows]) for c in range(count))
    left = (left * row_col_ref[...] * keep_left_ref[...]).astype(BF16)
    right = (right * row_row_ref[...] * keep_right_ref[...]).astype(BF16)

    @pl.when(step == 0)
    def _():
        left_ref[...] = left
        right_ref[...] = right

    @pl.when(step > 0)
    def _():
        left_ref[...] += left
        right_ref[...] += right


def columns(x, fill, row_col, row_row, keep_left, keep_right, weights, count):
    sources, owned, span, channels = x.shape
    rows = sources * span
    lanes = weights[-2].shape[2]

    def whole(a):
        return pl.BlockSpec(a.shape, lambda k, n=a.ndim: (0,) * n)

    column = pl.BlockSpec((sources, count, span, channels), lambda k: (0, k, 0, 0))
    smalls = (fill, row_col, row_row, keep_left, keep_right)
    specs = [column] + [whole(a) for a in smalls] + [whole(w) for w in weights[:-2]]
    specs += [pl.BlockSpec((count,) + w.shape[1:], lambda k: (k, 0, 0)) for w in weights[-2:]]
    return pl.pallas_call(
        column_kernel,
        grid=(owned // count,),
        in_specs=specs,
        out_specs=(
            column,
            pl.BlockSpec((rows, lanes), lambda k: (0, 0)),
            pl.BlockSpec((lanes, rows), lambda k: (0, 0)),
        ),
        out_shape=(
            jax.ShapeDtypeStruct(x.shape, BF16),
            jax.ShapeDtypeStruct((rows, lanes), BF16),
            jax.ShapeDtypeStruct((lanes, rows), BF16),
        ),
        scratch_shapes=[
            pltpu.VMEM((channels, count * rows), F32),
        ],
        compiler_params=pltpu.CompilerParams(
            dimension_semantics=("arbitrary",), vmem_limit_bytes=32 * 2**20
        ),
        cost_estimate=pl.CostEstimate(
            flops=6 * 10**9, bytes_accessed=4 * 2**20, transcendentals=4 * 10**6
        ),
    )(x, *smalls, *weights)


def pair_kernel(
    place_ref,
    pair_ref,
    scale_ref,
    left_ref,
    wo_ref,
    bias_ref,
    up_ref,
    down_ref,
    *refs,
    count,
):
    blocks = refs[: 2 * count]
    out_ref, flats, wo, tiles, made, in_sems, out_sems = refs[-7:]
    groups, rows, lanes = left_ref.shape
    width, near, _ = blocks[0].shape
    tall = width * near
    span = 2 * near
    cuts = lanes // COUPLING
    many = groups * span
    core = place_ref[count]
    spots = [pl.ds(pl.multiple_of(place_ref[n] * span, span), span) for n in range(count)]
    fetches = [pltpu.make_async_copy(wo_ref, wo, in_sems.at[count])]
    for n, spot in enumerate(spots):
        fetches.append(
            pltpu.make_async_copy(pair_ref.at[:, spot, :], tiles.at[n], in_sems.at[n])
        )
    for fetch in fetches:
        fetch.start()
    for n in range(count):
        own = blocks[2 * n][...].reshape(tall, rows)
        other = blocks[2 * n + 1][...].reshape(tall, rows)
        right = jnp.concatenate(
            [jnp.where(core == 0, own, other), jnp.where(core == 0, other, own)], axis=0
        )
        for pair in range(groups // 2):
            left = jnp.concatenate([left_ref[2 * pair], left_ref[2 * pair + 1]], axis=1)
            outer = dot(right, left)
            low, high = outer[:tall], outer[tall:]
            for half in range(2):
                cut = slice(half * lanes, (half + 1) * lanes)
                at = n * many + (2 * pair + half) * span
                for e in range(width):
                    part = slice(e * near, (e + 1) * near)
                    flats[at : at + span, e * lanes : (e + 1) * lanes] = jnp.concatenate(
                        [low[part, cut], high[part, cut]], axis=0
                    ).astype(BF16)
    for fetch in fetches:
        fetch.wait()
    projected = dot(flats[...], wo[...])
    bias = bias_ref[...]
    channels = bias.shape[1]
    stores = []
    for n, spot in enumerate(spots):
        kept = jnp.broadcast_to(scale_ref[spot, :], (span, channels))
        middle = []
        for g in range(groups):
            for k in range(cuts):
                i = g * cuts + k
                at = n * many + g * span
                block = projected[at : at + span, k * channels : (k + 1) * channels]
                scale = jnp.where(place_ref[count + 1 + i] > 0, kept, 1.0)
                middle.append(
                    (tiles[n, i].astype(F32) + (block + bias) * scale).astype(BF16)
                )
        middle = jnp.concatenate(middle, axis=0).astype(F32)
        normed = layer_norm(middle).astype(BF16)
        hidden = jnp.maximum(dot(normed, up_ref[...]), 0.0).astype(BF16)
        update = (middle + dot(hidden, down_ref[...])).astype(BF16)
        made[n] = update.reshape(groups * cuts, span, channels)
        stores.append(pltpu.make_async_copy(made.at[n], out_ref.at[:, spot, :], out_sems.at[n]))
        stores[-1].start()
    for store in stores:
        store.wait()


def pair_blocks(place, pair, scale, left, weights, blocks, before):
    count = len(blocks) // 2
    _, near, rows = blocks[0].shape
    groups, _, lanes = left.shape

    def whole(a):
        return pl.BlockSpec(a.shape, lambda i, place, n=a.ndim: (0,) * n)

    operands = [pair, scale, left, *weights, *blocks, *before]
    far = pl.BlockSpec(memory_space=pl.ANY)
    specs = [whole(a) for a in operands]
    for n in (0, 3, *range(len(operands) - len(before), len(operands))):
        specs[n] = far
    span = 2 * near
    tiles = pltpu.VMEM((count, pair.shape[0], span, pair.shape[2]), pair.dtype)
    return pl.pallas_call(
        functools.partial(pair_kernel, count=count),
        grid_spec=pltpu.PrefetchScalarGridSpec(
            num_scalar_prefetch=1,
            grid=(1,),
            in_specs=specs,
            out_specs=far,
            scratch_shapes=[
                pltpu.VMEM((count * groups * span, COUPLING * lanes), BF16),
                pltpu.VMEM(weights[0].shape, BF16),
                tiles,
                tiles,
                pltpu.SemaphoreType.DMA((count + 1,)),
                pltpu.SemaphoreType.DMA((count,)),
            ],
        ),
        out_shape=jax.ShapeDtypeStruct(pair.shape, pair.dtype),
        input_output_aliases={len(operands): 0} if before else {},
        compiler_params=pltpu.CompilerParams(
            dimension_semantics=("arbitrary",), vmem_limit_bytes=36 * 2**20
        ),
        cost_estimate=pl.CostEstimate(
            flops=count * 2 * 10**9, bytes_accessed=6 * 2**20, transcendentals=0
        ),
    )(place, *operands)


NEWPAIR = True


def ring(size, shift):
    return [(i, (i + shift) % size) for i in range(size)]


def left_route(sizes):
    zs, ys, cs, xs, ls = sizes
    pairs = []
    place = lambda z, y, c, x, l: (((z * ys + y) * cs + c) * xs + x) * ls + l
    for z in range(zs):
        for y in range(ys):
            for c in range(cs):
                for x in range(xs):
                    for l in range(ls):
                        block = z // 2
                        slot = 4 * (z % 2) + 2 * c + y
                        pairs.append(
                            (
                                place(z, y, c, x, l),
                                place(x * ls + l, block // cs, block % cs, slot // ls, slot % ls),
                            )
                        )
    return pairs


def per_device(
    homolog_embedding,
    pair_features,
    row_present_mask,
    residue_keep_mask,
    query_weight,
    key_weight,
    content_matrix,
    sigmoid_switch_matrix,
    focus_merge_matrix,
    widening_matrix,
    narrowing_matrix,
    first_factor_matrix,
    second_factor_matrix,
    outer_product_weight,
    outer_product_bias,
    pair_up_weight,
    pair_down_weight,
):
    sizes = tuple(lax.axis_size(a) for a in SEQ + RES)
    zs, ys, cs, xs, ls = sizes
    z, yh, co, xi, li = (lax.axis_index(a) for a in SEQ + RES)
    span, breadth, channels = homolog_embedding.shape
    seq_count, res_count = zs * ys * cs, xs * ls
    owned = breadth // seq_count
    rows = span * seq_count
    pair_rows, _, pair_channels = pair_features.shape
    res_index = xi * ls + li
    seq_index = (z * ys + yh) * cs + co
    flags = row_present_mask.astype(F32)
    keep = residue_keep_mask.astype(F32)

    x = homolog_embedding.reshape(span, zs, cs, ys, owned, channels)
    x = x.transpose(1, 3, 2, 4, 0, 5).reshape(seq_count, owned, span, channels)
    x = lax.all_to_all(x, SEQ, split_axis=0, concat_axis=0, tiled=True)

    row_keep = lax.dynamic_slice_in_dim(
        residue_keep_mask, seq_index * pair_rows, pair_rows, 0
    )
    col_keep = lax.dynamic_slice_in_dim(keep, res_index * breadth, breadth, 0)
    scale = (1.0 / jnp.maximum(jnp.sum(flags) * col_keep, 1.0))[:, None]
    wo = outer_product_weight.reshape(COUPLING, COUPLING, pair_channels).transpose(1, 0, 2)
    wo = jnp.where(
        (jnp.arange(owned)[:, None] == jnp.arange(owned)[None, :])[None, :, None, :, None],
        wo[:, None, :, None, :],
        jnp.zeros((), BF16),
    ).reshape(COUPLING * owned * COUPLING, owned * pair_channels)
    steps = (0, *(s * k for k in range(1, zs // 2) for s in (-1, 1)), zs // 2)
    places = jnp.stack([(z + k + zs) % zs for k in steps])
    places = [
        jnp.concatenate([part, co[None], row_keep]).astype(jnp.int32)
        for part in (places[:EARLY], places[EARLY:])
    ]
    x, wo, scale, places = lax.optimization_barrier((x, wo, scale, places))

    first = res_index * breadth + ((z * cs + co) * ys + yh) * owned
    mine = lax.dynamic_slice_in_dim(keep, first, owned, 0)
    keep_left = jnp.repeat(mine, COUPLING)[None, :]
    keep_right = jnp.tile(mine, COUPLING)[:, None]
    pad_left = jnp.zeros((owned, channels, owned, COUPLING), BF16)
    pad_right = jnp.zeros((owned, COUPLING, owned, channels), BF16)
    for k in range(owned):
        pad_left = pad_left.at[k, :, k].set(first_factor_matrix)
        pad_right = pad_right.at[k, :, k].set(second_factor_matrix.T)
    weights = (
        query_weight.T,
        key_weight,
        content_matrix.T,
        sigmoid_switch_matrix,
        focus_merge_matrix,
        widening_matrix,
        narrowing_matrix,
        pad_left.reshape(owned, channels, owned * COUPLING),
        pad_right.reshape(owned, COUPLING * owned, channels),
    )
    fill = ((flags - 1.0) * MASK_FILL)[:, None]
    update, left, right = columns(
        x,
        fill,
        flags[:, None],
        flags[None, :],
        keep_left,
        keep_right,
        weights,
        owned // PARTS,
    )

    left = lax.ppermute(left, SEQ + RES, left_route(sizes))

    right = right.reshape(COUPLING, owned, rows)
    away = lax.ppermute(right, "yh", ring(ys, 1))
    right = jnp.where(
        yh == 0,
        jnp.concatenate([right, away], axis=1),
        jnp.concatenate([away, right], axis=1),
    )
    up = down = right
    blocks = [right]
    for k in range(1, zs // 2):
        if k == TIE:
            left, up, down = lax.optimization_barrier((left, up, down))
        up = lax.ppermute(up, "z", ring(zs, 1))
        down = lax.ppermute(down, "z", ring(zs, -1))
        blocks += [up, down]
    left = jnp.broadcast_to(left[None], (res_count, *left.shape))
    left = lax.all_to_all(left, RES, split_axis=0, concat_axis=0, tiled=True)
    left, up, down = lax.optimization_barrier((left, up, down))
    left, update = lax.optimization_barrier((left, update))
    update = lax.all_to_all(update, SEQ, split_axis=0, concat_axis=0, tiled=True)
    update = update.reshape(zs, ys, cs, owned, span, channels).transpose(4, 0, 2, 1, 3, 5)
    update = update.reshape(span, breadth, channels)
    half = COUPLING // 2
    up = lax.ppermute(up[:half], "z", ring(zs, 1))
    down = lax.ppermute(down[half:], "z", ring(zs, -1))
    blocks = [(own, lax.ppermute(own, "co", ring(cs, 1))) for own in blocks]

    pair_weights = (wo, outer_product_bias[None, :], pair_up_weight, pair_down_weight)

    def tiles(place, few, before):
        few = [block for own, other in few for block in (own, other)]
        return pair_blocks(place, pair_features, scale, left, pair_weights, few, before)

    pair = tiles(places[0], blocks[:EARLY], ())
    up, down, pair = lax.optimization_barrier((up, down, pair))
    own = jnp.concatenate([up, down], axis=0)
    blocks.append((own, lax.ppermute(own, "co", ring(cs, 1))))
    pair = tiles(places[1], blocks[EARLY:], (pair,))
    return update, pair


def solution(mesh):
    grid = mesh.devices.reshape(8, 2, 2, 4, 2)
    fine = Mesh(grid, SEQ + RES)
    split = P(SEQ, RES, None)
    return jax.shard_map(
        per_device,
        mesh=fine,
        in_specs=(split, split) + (P(),) * 15,
        out_specs=(split, split),
        check_vma=False,
    )
```
